128 devices in a mesh: group: 4 (over y), batch: 32 (over z, x, core).
Axes of the slice: x: 4, y: 4, z: 4, core: 2. Of those that a mesh axis runs over, the one named last changes fastest.
Arguments:
- queries: bfloat16 [49152, 256], P(('group', 'batch')), may hold values from -20 to 20
- pos_emb: bfloat16 [49152, 256], P(('group', 'batch')), may hold values from -6 to 6
- pos_logq: bfloat16 [49152], P(('group', 'batch')), may hold values from -14 to -11
- pos_ids: int32 [49152], P(('group', 'batch')), may hold values from 0 to 8388607
- row_weight: float32 [49152], P(('group', 'batch')), may hold values from 1 to 16
- neg_emb: bfloat16 [16384, 256], P(('group', 'batch')), may hold values from -5 to 5
- neg_logq: bfloat16 [16384], P(('group', 'batch')), may hold values from -14 to -11
- neg_ids: int32 [16384], P(('group', 'batch')), may hold values from 0 to 8388607
- neg_owner: int32 [16384], P(('group', 'batch')), may hold values from 0 to 3, as said below
- neg_slot: int32 [16384], P(('group', 'batch')), may hold values from 0 to 511
Outputs:
- query_grad: float32 [49152, 256], P(('group', 'batch'))
- item_grad: float32 [49152, 256], P(('group', 'batch'))
- table_grad: float32 [65536, 256], P(('group', 'batch'))
The draws below stay inside these ranges and needn't reach their ends.
Inputs may be any that keep to these rules, and one draw needn't show every extreme that they name: `neg_owner`: each device sends exactly 64 of its sampled rows to one owner group, the same group for all devices with the same batch index, and its other rows to the other groups.
All inputs are finite; a program needn't handle non-finite values.
Results may differ from the reference program's by a relative error of at most 0.0035.
Values may be sent and summed in bfloat16 or wider, within the bound.
A program may use at most 128 MiB of HBM per device.

```python
import math
import jax
import jax.numpy as jnp
from jax import lax

D = 256
TOK_DEV = 384
NEG_DEV = 128
SLOTS = 512
ITEMS = 8388608
TOKENS = 49152
NEGS = 16384
TABLE = 65536
N_GROUP = 4
N_BATCH = 32


def draw_towers(key):
    keys = jax.random.split(key, 2)
    shape = (TOKENS, D)
    normal_q = jnp.clip(jax.random.normal(keys[0], shape, jnp.float32), -5.0, 5.0)
    normal_p = jnp.clip(jax.random.normal(keys[1], shape, jnp.float32), -5.0, 5.0)
    base_q = normal_q
    base_p = normal_p
    return (base_q, base_p)


def draw_queries(key, part):
    base_q, base_p = draw_towers(key)
    return base_q.astype(jnp.bfloat16)


def draw_pos_emb(key, part):
    base_q, base_p = draw_towers(key)
    return base_p.astype(jnp.bfloat16)


def popular_items(key):
    return jax.random.randint(jax.random.fold_in(key, 5), (16,), 0, ITEMS)


def mixed_ids(key, count, popular):
    keys = jax.random.split(key, 3)
    pick = jax.random.randint(keys[0], (count,), 0, 16)
    fresh = jax.random.randint(keys[1], (count,), 0, ITEMS)
    use_popular = jax.random.randint(keys[2], (count,), 0, 2) == 0
    popular_rows = jnp.sum(jnp.where(pick[:, None] == jnp.arange(16)[None, :], popular[None, :], 0), axis=1)
    return jnp.where(use_popular, popular_rows, fresh).astype(jnp.int32)


def draw_pos_ids(key, part):
    popular = popular_items(key)
    key = jax.random.fold_in(key, 21)
    return mixed_ids(key, TOKENS, popular)


def draw_neg_ids(key, part):
    popular = popular_items(key)
    key = jax.random.fold_in(key, 22)
    return mixed_ids(key, NEGS, popular)


def draw_neg_owner(key, part):
    key = jax.random.fold_in(key, 11)
    keys = jax.random.split(key, 3)
    device_count = N_GROUP * N_BATCH
    hot_group = jax.random.randint(keys[0], (N_BATCH,), 0, N_GROUP)
    shuffled = jax.vmap(lambda sub: jax.random.permutation(sub, NEG_DEV))(jax.random.split(keys[1], device_count))
    device_index = jnp.arange(device_count)
    hot_rows = hot_group[device_index % N_BATCH][:, None]
    elsewhere = (hot_rows + 1 + jax.random.randint(keys[2], (device_count, NEG_DEV), 0, N_GROUP - 1)) % N_GROUP
    owners = jnp.where(shuffled < NEG_DEV // 2, hot_rows, elsewhere)
    return owners.reshape(-1).astype(jnp.int32)


def with_ends(result, own_key, low, top_value):
    longest = result.shape.index(max(result.shape))
    spots = []
    for shift in (0, 1):
        where = [jax.random.randint(jax.random.fold_in(own_key, axis), (), 0, length) for axis, length in enumerate(result.shape)]
        where[longest] = (where[longest] + shift) % result.shape[longest]
        spots.append(tuple(where))
    return result.at[spots[0]].set(low).at[spots[1]].set(top_value)


def block_levels(key, shape, pieces, smallest, high):
    def one(position, shards_of):
        steps = jax.random.uniform(jax.random.fold_in(jax.random.fold_in(key, 6), position), (shards_of,), jnp.float32, smallest / len(pieces), high / len(pieces))
        return jnp.repeat(jnp.exp(steps), shape[position] // shards_of).reshape((-1,) + (1,) * (len(shape) - position - 1))

    level = one(*pieces[0])
    for cut in pieces[1:]:
        level = level * one(*cut)
    return level


def gaussian(rng, dims, spread, limit, pieces=(), kind=jnp.bfloat16):
    array = spread * jax.random.normal(rng, dims, jnp.float32)
    if pieces:
        array = array * block_levels(rng, dims, pieces, -0.22, 0.18)
    return jnp.clip(array, -limit, limit).astype(kind)


def setup_inputs(seed: int = 0) -> dict:
    splits = jax.random.split(jax.random.key(seed), 11)
    return {
        "queries": draw_queries(jax.random.fold_in(splits[10], 71), 0),
        "pos_emb": draw_pos_emb(jax.random.fold_in(splits[10], 71), 0),
        "pos_logq": jnp.clip(-14.0 + 3.0 * jax.random.uniform(splits[2], (TOKENS,), jnp.float32) ** block_levels(splits[2], (TOKENS,), ((0, 128),), -0.2, 0.2), -14.0, -11.0).astype(jnp.bfloat16),
        "pos_ids": draw_pos_ids(jax.random.fold_in(splits[10], 71), 0),
        "row_weight": jnp.clip(jnp.exp(math.log(16.0) - 2.7725887 * jax.random.uniform(splits[4], (TOKENS,), jnp.float32) ** block_levels(splits[4], (TOKENS,), ((0, 128),), -0.2, 0.2)), 1.0, 16.0),
        "neg_emb": gaussian(splits[5], (NEGS, D), 1.0, 5.0, ((0, 128),)),
        "neg_logq": jnp.clip(-14.0 + 3.0 * jax.random.uniform(splits[6], (NEGS,), jnp.float32) ** block_levels(splits[6], (NEGS,), ((0, 128),), -0.2, 0.2), -14.0, -11.0).astype(jnp.bfloat16),
        "neg_ids": draw_neg_ids(jax.random.fold_in(splits[10], 71), 0),
        "neg_owner": draw_neg_owner(jax.random.fold_in(splits[10], 71), 0),
        "neg_slot": with_ends(jax.random.randint(splits[9], (NEGS,), 0, SLOTS), jax.random.fold_in(splits[9], 1), 0, SLOTS - 1).astype(jnp.int32),
    }


score_scale = 0.125


def reference(queries, pos_emb, pos_logq, pos_ids, row_weight, neg_emb, neg_logq, neg_ids, neg_owner, neg_slot):
    groups = N_GROUP
    shards = N_BATCH
    per_device = TOK_DEV + NEG_DEV
    cand_count = shards * per_device
    query_blocks = queries.reshape(groups, shards, TOK_DEV, D)
    candidates = jnp.concatenate([pos_emb.reshape(groups, shards, TOK_DEV, D), neg_emb.reshape(groups, shards, NEG_DEV, D)], axis=2).reshape(groups, cand_count, D)
    cand_logq = jnp.concatenate([pos_logq.reshape(groups, shards, TOK_DEV), neg_logq.reshape(groups, shards, NEG_DEV)], axis=2).reshape(groups, cand_count).astype(jnp.float32)
    cand_ids = jnp.concatenate([pos_ids.reshape(groups, shards, TOK_DEV), neg_ids.reshape(groups, shards, NEG_DEV)], axis=2).reshape(groups, cand_count)
    weights = row_weight.reshape(groups, shards, TOK_DEV)
    row_ids = pos_ids.reshape(groups, shards, TOK_DEV)
    cand_index = jnp.arange(cand_count, dtype=jnp.int32)
    local_rows = jnp.arange(TOK_DEV, dtype=jnp.int32)

    def one_group(group_inputs):
        group_queries, group_cands, group_logq, group_ids, group_weights, group_rows = group_inputs

        def one_device(running, device_inputs):
            dev_queries, dev_weights, dev_ids, batch_pos = device_inputs
            targets = batch_pos * per_device + local_rows
            scores = jnp.dot(dev_queries, group_cands.T, preferred_element_type=jnp.float32) * score_scale - group_logq[None, :]
            is_target = cand_index[None, :] == targets[:, None]
            allowed = jnp.logical_or(group_ids[None, :] != dev_ids[:, None], is_target)
            row_max = jnp.max(jnp.where(allowed, scores, -jnp.inf), axis=1, keepdims=True)
            row_lse = row_max + jnp.log(jnp.sum(jnp.where(allowed, jnp.exp(scores - row_max), 0.0), axis=1, keepdims=True))
            soft_weights = jnp.where(allowed, jnp.exp(scores - row_lse), 0.0)
            grad_logits = (dev_weights[:, None] * (soft_weights - is_target.astype(jnp.float32))).astype(jnp.bfloat16)
            query_part = jnp.dot(grad_logits, group_cands, preferred_element_type=jnp.float32) * score_scale
            running = running + jnp.dot(grad_logits.T, dev_queries, preferred_element_type=jnp.float32) * score_scale
            return running, query_part

        zero_grads = jnp.zeros((cand_count, D), jnp.float32)
        return lax.scan(one_device, zero_grads, (group_queries, group_weights, group_rows, jnp.arange(shards, dtype=jnp.int32)))

    cand_grads, query_parts = lax.map(one_group, (query_blocks, candidates, cand_logq, cand_ids, weights, row_ids))
    cand_grads = cand_grads.reshape(groups, shards, per_device, D)
    item_grad = cand_grads[:, :, :TOK_DEV].reshape(TOKENS, D)
    sampled_grad = cand_grads[:, :, TOK_DEV:].reshape(NEGS, D)
    sender = jnp.arange(NEGS, dtype=jnp.int32) // NEG_DEV
    table_rows = (neg_owner * shards + sender % shards) * SLOTS + neg_slot
    table_grad = jnp.zeros((TABLE, D), jnp.float32).at[table_rows].add(sampled_grad)
    return query_parts.reshape(TOKENS, D), item_grad, table_grad
```

```python
import functools
import math

import jax
import jax.numpy as jnp
from jax import lax
from jax.experimental import pallas as pl
from jax.experimental.pallas import tpu as pltpu
from jax.sharding import PartitionSpec as P

MESH = pl.DeviceIdType.MESH
F32 = jnp.float32
BF16 = jnp.bfloat16
LOG2E = math.log2(math.e)
SCALE = 0.125
FLOOR = -1e30

ROWS = 384
NEGS = 128
CANDS = ROWS + NEGS
PAIR = 2 * ROWS
DIM = 256
SLOTS = 512
CHUNK = 32

DIST = (0, 1, 3, 2)
PLACE = (0, 1, 3, 2)


def tiled(x, count):
    return jnp.concatenate([x] * count, axis=1)


def kernel(
    q_in, pos_in, neg_in, cmeta_in, qmeta_in, ymeta_in,
    qgt_out, item_out, table_out,
    cands, cands_t, quers, scores, weights,
    cmeta, qmeta, ymeta, logq_col, id_col, stat, stats, shift,
    cand_part, cand_send, cand_relay, cand_got,
    quer_part, sib_send, sib_got, quer_send, quer_relay, quer_got,
    neg_rows, onehot, local_sem, send_sem, recv_sem,
):
    g = lax.axis_index("group")
    b = lax.axis_index("batch")
    z, x, c = b // 8, (b // 2) % 4, b % 2
    my_abs = x * 2 + c

    def along_z(step):
        return {"batch": ((z + step) % 4) * 8 + x * 2 + c}

    def along_x(step, flip=0):
        core = (1 - c) if flip else c
        return {"batch": z * 8 + ((x + step) % 4) * 2 + core}

    def along_y(step):
        return {"group": (g + step) % 4}

    sems = iter(range(64))
    sent = []

    def remote(src, dst, target, k=None):
        k = next(sems) if k is None else k
        return pltpu.make_async_remote_copy(
            src_ref=src, dst_ref=dst, send_sem=send_sem.at[k], recv_sem=recv_sem.at[k],
            device_id=target, device_id_type=MESH,
        )

    def go(copy):
        copy.start()
        sent.append(copy)

    locals_ = [
        pltpu.make_async_copy(q_in, quers.at[0, pl.ds(0, ROWS)], local_sem.at[0]),
        pltpu.make_async_copy(pos_in, cands.at[0, pl.ds(0, ROWS)], local_sem.at[1]),
        pltpu.make_async_copy(neg_in, cands.at[0, pl.ds(ROWS, NEGS)], local_sem.at[2]),
    ]
    for copy in locals_:
        copy.start()
    cmeta[0] = cmeta_in[...]
    qmeta[0, :, 0:ROWS] = qmeta_in[...]
    ymeta[0] = ymeta_in[...]

    peers = [along_z(s) for s in (1, 2, 3)]
    peers += [along_x(s, f) for s in range(4) for f in range(2) if (s, f) != (0, 0)]
    peers += [along_y(s) for s in (1, 2, 3)]
    barrier = pltpu.get_barrier_semaphore()
    for peer in peers:
        pl.semaphore_signal(barrier, inc=1, device_id=peer, device_id_type=MESH)
    pl.semaphore_wait(barrier, len(peers))

    qmeta_copies = {}
    for s in range(4):
        for f in range(2):
            if (s, f) != (0, 0):
                place = qmeta.at[PLACE[s], :, pl.ds(f * ROWS, ROWS)]
                qmeta_copies[(PLACE[s], f)] = remote(qmeta.at[0, :, pl.ds(0, ROWS)], place, along_x(s, f))
    cmeta_copies = {PLACE[s]: remote(cmeta.at[0], cmeta.at[PLACE[s]], along_z(s)) for s in (1, 2, 3)}
    ymeta_copies = [remote(ymeta.at[0], ymeta.at[s], along_y(s)) for s in (1, 2, 3)]
    for copy in (*qmeta_copies.values(), *cmeta_copies.values(), *ymeta_copies):
        go(copy)
    for copy in locals_:
        copy.wait()

    qh, ch = ROWS // 2, CANDS // 2

    def quer_at(p, half):
        return quers.at[p, pl.ds(half * qh, qh)]

    def cand_at(p, half):
        return cands.at[p, pl.ds(half * ch, ch)]

    sib = [
        remote(quers.at[p, pl.ds(0, ROWS)], quers.at[p, pl.ds(ROWS, ROWS)], along_x(0, 1)) for p in range(4)
    ]
    quer_up = [remote(quer_at(0, h), quer_at(1, h), along_x(1)) for h in (0, 1)]
    quer_down = [remote(quer_at(0, h), quer_at(2, h), along_x(-1)) for h in (0, 1)]
    quer_far = [
        remote(quer_at(1, 0), quer_at(3, 0), along_x(1)),
        remote(quer_at(2, 1), quer_at(3, 1), along_x(-1)),
    ]
    cand_up = [remote(cand_at(0, h), cand_at(1, h), along_z(1)) for h in (0, 1)]
    cand_down = [remote(cand_at(0, h), cand_at(2, h), along_z(-1)) for h in (0, 1)]
    cand_far = [
        remote(cand_at(1, 0), cand_at(3, 0), along_z(1)),
        remote(cand_at(2, 1), cand_at(3, 1), along_z(-1)),
    ]
    go(sib[0])
    go(quer_up[0])
    go(quer_down[1])
    go(cand_up[0])
    go(cand_down[1])
    go(quer_up[1])
    go(quer_down[0])
    go(cand_up[1])
    go(cand_down[0])

    stat[...] = jnp.concatenate(
        [jnp.full((4, 1, PAIR), FLOOR, F32), jnp.zeros((4, 1, PAIR), F32)], axis=0
    )

    def columns(p):
        for k in range(CANDS // 128):
            lanes = pl.ds(k * 128, 128)
            for row, ref in ((0, logq_col), (1, id_col)):
                ref[p, lanes, :] = jnp.broadcast_to(cmeta[p, row : row + 1, lanes], (128, 128)).T

    def on_target(r):
        r_index = lax.broadcasted_iota(jnp.int32, (CHUNK, PAIR), 0) + r * CHUNK
        q_index = lax.broadcasted_iota(jnp.int32, (CHUNK, PAIR), 1)
        return jnp.logical_and(r_index == q_index, q_index < ROWS)

    def tile(p, cs, diagonal):
        scores[p, cs] = lax.dot_general(
            cands[cs], quers[p], (((1,), (1,)), ((), ())), preferred_element_type=F32
        )
        row_ids = qmeta[p, 0:1, :]

        def mask(r, peak):
            rows = pl.ds(pl.multiple_of(r * CHUNK, CHUNK), CHUNK)
            s = scores[p, cs, rows, :] * (SCALE * LOG2E) - tiled(logq_col[cs, rows, :], PAIR // 128)
            drop = tiled(id_col[cs, rows, :], PAIR // 128) == row_ids
            if diagonal:
                drop = jnp.logical_and(drop, jnp.logical_not(on_target(r)))
            s = jnp.where(drop, FLOOR, s)
            scores[p, cs, rows, :] = s
            return jnp.maximum(peak, jnp.max(s.reshape(CHUNK // 8, 8, PAIR), axis=0))

        peak = lax.fori_loop(0, CANDS // CHUNK, mask, jnp.full((8, PAIR), FLOOR, F32), unroll=True)
        old = stat[p]
        new = jnp.maximum(old, jnp.max(peak, axis=0, keepdims=True))

        def add(r, total):
            rows = pl.ds(pl.multiple_of(r * CHUNK, CHUNK), CHUNK)
            e = jnp.exp2(scores[p, cs, rows, :] - new)
            return total + jnp.sum(e.reshape(CHUNK // 8, 8, PAIR), axis=0)

        total = lax.fori_loop(0, CANDS // CHUNK, add, jnp.zeros((8, PAIR), F32), unroll=True)
        stat[p] = new
        stat[4 + p] = stat[4 + p] * jnp.exp2(old - new) + jnp.sum(total, axis=0, keepdims=True)

    def tiles(p_first, p_count, c_first, c_count):
        @pl.loop(0, p_count * c_count)
        def _(t):
            tile(p_first + t % p_count, c_first + t // p_count, False)

    columns(0)
    sib[0].wait_recv()
    qmeta_copies[(0, 1)].wait_recv()
    tile(0, 0, True)
    quer_up[0].wait_recv()
    go(quer_far[0])
    quer_down[1].wait_recv()
    go(quer_far[1])
    cand_up[0].wait_recv()
    go(cand_far[0])
    cand_down[1].wait_recv()
    go(cand_far[1])
    quer_up[1].wait_recv()
    go(sib[1])
    quer_down[0].wait_recv()
    go(sib[2])
    sib[1].wait_recv()
    sib[2].wait_recv()
    for p in (1, 2):
        for f in (0, 1):
            qmeta_copies[(p, f)].wait_recv()
    tiles(1, 2, 0, 1)
    quer_far[0].wait_recv()
    quer_far[1].wait_recv()
    go(sib[3])
    cand_up[1].wait_recv()
    cand_down[0].wait_recv()
    for p in (1, 2):
        cmeta_copies[p].wait_recv()
        columns(p)
    tiles(0, 3, 1, 2)
    sib[3].wait_recv()
    for f in (0, 1):
        qmeta_copies[(3, f)].wait_recv()
    tiles(3, 1, 0, 3)
    cand_far[0].wait_recv()
    cand_far[1].wait_recv()
    cmeta_copies[3].wait_recv()
    columns(3)
    tiles(0, 4, 3, 1)

    def owner(p, f):
        core = (1 - c) if f else c
        return ((x + 4 - DIST[p]) % 4) * 2 + core

    for p in range(4):
        for f in range(2):
            row = pl.ds(owner(p, f), 1)
            lanes = slice(f * ROWS, (f + 1) * ROWS)
            stats[my_abs, 0, row, :] = stat[p][:, lanes]
            stats[my_abs, 1, row, :] = stat[4 + p][:, lanes]
    stat_copies = []
    for s in range(4):
        for f in range(2):
            if (s, f) != (0, 0):
                j = next(sems)
                go(remote(stats.at[my_abs], stats.at[my_abs], along_x(s, f), j))
                k = owner(PLACE[s], f)
                stat_copies.append(remote(stats.at[k], stats.at[k], along_x(s, f), j))
    for cs in range(4):
        cands_t[:, cs * CANDS : (cs + 1) * CANDS] = cands[cs].T
    for copy in stat_copies:
        copy.wait_recv()
    peak = stats[0, 0]
    for k in range(1, 8):
        peak = jnp.maximum(peak, stats[k, 0])
    total = jnp.zeros_like(peak)
    for k in range(8):
        total = total + stats[k, 1] * jnp.exp2(stats[k, 0] - peak)
    shift[...] = peak + jnp.log(total) * LOG2E
    lifts = []
    for p in range(4):
        lse = jnp.concatenate([shift[pl.ds(owner(p, f), 1), :] for f in range(2)], axis=1)
        lifts.append(jnp.log(qmeta[p, 1:2, :]) * LOG2E - lse)

    def cand_block(cs):
        @pl.loop(0, CANDS // CHUNK, unroll=4)
        def _(r):
            rows = pl.ds(pl.multiple_of(r * CHUNK, CHUNK), CHUNK)
            out = pl.ds(pl.multiple_of(cs * CANDS + r * CHUNK, CHUNK), CHUNK)
            for p in range(4):
                gw = jnp.exp2(scores[p, cs, rows, :] + lifts[p])
                if p == 0 and cs == 0:
                    gw = jnp.where(on_target(r), gw - qmeta[0, 1:2, :], gw)
                weights[out, p * PAIR : (p + 1) * PAIR] = gw.astype(BF16)

        cand_part[cs] = jnp.dot(
            weights[cs * CANDS : (cs + 1) * CANDS, :], quers[...].reshape(4 * PAIR, DIM),
            preferred_element_type=F32,
        )

    up, low = pl.ds(0, ch), pl.ds(ch, ch)
    relay_copies = [
        remote(cand_send.at[2, up], cand_relay.at[0], along_z(-1)),
        remote(cand_send.at[2, low], cand_relay.at[1], along_z(1)),
    ]
    to_down = [remote(cand_send.at[0, h], cand_got.at[0, h], along_z(-1)) for h in (up, low)]
    to_up = [remote(cand_send.at[1, h], cand_got.at[1, h], along_z(1)) for h in (up, low)]
    cand_block(3)
    cand_send[2] = cand_part[3].astype(BF16)
    go(relay_copies[1])
    go(relay_copies[0])
    cand_block(1)
    cand_send[0, low, :] = cand_part[1, low, :].astype(BF16)
    go(to_down[1])
    cand_block(2)
    cand_send[1, up, :] = cand_part[2, up, :].astype(BF16)
    go(to_up[0])
    relay_copies[1].wait_recv()
    cand_send[1, low, :] = (cand_part[2, low, :] + cand_relay[1].astype(F32)).astype(BF16)
    go(to_up[1])
    relay_copies[0].wait_recv()
    cand_send[0, up, :] = (cand_part[1, up, :] + cand_relay[0].astype(F32)).astype(BF16)
    go(to_down[0])
    cand_block(0)

    def quer_block(p):
        quer_part[p] = jnp.dot(
            cands_t[...], weights[:, p * PAIR : (p + 1) * PAIR], preferred_element_type=F32
        )
        sib_send[p] = quer_part[p, :, ROWS:PAIR].astype(BF16)
        go(sib_parts[p])

    def summed(p, rows):
        return quer_part[p, rows, 0:ROWS] + sib_got[p, rows, :].astype(F32)

    sib_parts = [remote(sib_send.at[p], sib_got.at[p], along_x(0, 1)) for p in range(4)]
    qup, qlow = pl.ds(0, DIM // 2), pl.ds(DIM // 2, DIM // 2)
    quer_relays = [
        remote(quer_send.at[2, qup], quer_relay.at[0], along_x(-1)),
        remote(quer_send.at[2, qlow], quer_relay.at[1], along_x(1)),
    ]
    q_down = [remote(quer_send.at[0, h], quer_got.at[0, h], along_x(-1)) for h in (qup, qlow)]
    q_up = [remote(quer_send.at[1, h], quer_got.at[1, h], along_x(1)) for h in (qup, qlow)]
    quer_block(3)
    quer_block(1)
    sib_parts[3].wait_recv()
    quer_send[2] = summed(3, slice(None)).astype(BF16)
    go(quer_relays[0])
    go(quer_relays[1])
    quer_block(2)
    sib_parts[1].wait_recv()
    quer_send[0, qlow, :] = summed(1, qlow).astype(BF16)
    go(q_down[1])
    quer_block(0)
    sib_parts[2].wait_recv()
    quer_send[1, qup, :] = summed(2, qup).astype(BF16)
    go(q_up[0])
    quer_relays[0].wait_recv()
    quer_send[0, qup, :] = (summed(1, qup) + quer_relay[0].astype(F32)).astype(BF16)
    go(q_down[0])
    quer_relays[1].wait_recv()
    quer_send[1, qlow, :] = (summed(2, qlow) + quer_relay[1].astype(F32)).astype(BF16)
    go(q_up[1])

    to_down[1].wait_recv()
    to_up[1].wait_recv()
    negs = pl.ds(ROWS, NEGS)
    neg_rows[0] = (
        cand_part[0, negs, :] + cand_got[0, negs, :].astype(F32) + cand_got[1, negs, :].astype(F32)
    )
    neg_copies = [remote(neg_rows.at[0], neg_rows.at[s], along_y(s)) for s in (1, 2, 3)]
    for copy in neg_copies:
        go(copy)
    to_down[0].wait_recv()
    to_up[0].wait_recv()
    item = pl.ds(0, ROWS)
    item_out[...] = (
        cand_part[0, item, :] + cand_got[0, item, :].astype(F32) + cand_got[1, item, :].astype(F32)
    )
    for copy in ymeta_copies:
        copy.wait_recv()
    for k in range(4):
        want = lax.broadcasted_iota(jnp.int32, (SLOTS, NEGS), 0) + g * SLOTS
        onehot[:, k * NEGS : (k + 1) * NEGS] = jnp.where(ymeta[k] == want, 1.0, 0.0).astype(BF16)

    sib_parts[0].wait_recv()
    for copy in (*q_down, *q_up):
        copy.wait_recv()
    qgt_out[...] = summed(0, slice(None)) + quer_got[0].astype(F32) + quer_got[1].astype(F32)

    for copy in neg_copies:
        copy.wait_recv()
    rows = neg_rows[...].reshape(4 * NEGS, DIM)
    high = rows.astype(BF16)
    rest = (rows - high.astype(F32)).astype(BF16)
    table_out[...] = jnp.dot(onehot[...], high, preferred_element_type=F32) + jnp.dot(
        onehot[...], rest, preferred_element_type=F32
    )
    for copy in sent:
        copy.wait_send()


def local(
    queries, pos_emb, pos_logq, pos_ids, row_weight, neg_emb, neg_logq, neg_ids, neg_owner, neg_slot
):
    cmeta = jnp.stack(
        [
            jnp.concatenate([pos_logq, neg_logq]).astype(F32) * LOG2E,
            jnp.concatenate([pos_ids, neg_ids]).astype(F32),
        ]
    )
    qmeta = jnp.stack([pos_ids.astype(F32), row_weight])
    ymeta = (neg_owner * SLOTS + neg_slot).reshape(1, NEGS)
    whole = pl.BlockSpec(memory_space=pltpu.VMEM)
    far = pl.BlockSpec(memory_space=pl.ANY)
    vmem = pltpu.VMEM
    query_grad_t, item_grad, table_grad = pl.pallas_call(
        kernel,
        out_shape=[
            jax.ShapeDtypeStruct((DIM, ROWS), F32),
            jax.ShapeDtypeStruct((ROWS, DIM), F32),
            jax.ShapeDtypeStruct((SLOTS, DIM), F32),
        ],
        in_specs=[far, far, far, whole, whole, whole],
        out_specs=[whole, whole, whole],
        scratch_shapes=[
            vmem((4, CANDS, DIM), BF16),
            vmem((DIM, 4 * CANDS), BF16),
            vmem((4, PAIR, DIM), BF16),
            vmem((4, 4, CANDS, PAIR), F32),
            vmem((4 * CANDS, 4 * PAIR), BF16),
            vmem((4, 2, CANDS), F32),
            vmem((4, 2, PAIR), F32),
            vmem((4, 1, NEGS), jnp.int32),
            vmem((4, CANDS, 128), F32),
            vmem((4, CANDS, 128), F32),
            vmem((8, 1, PAIR), F32),
            vmem((8, 2, 8, ROWS), F32),
            vmem((8, ROWS), F32),
            vmem((4, CANDS, DIM), F32),
            vmem((3, CANDS, DIM), BF16),
            vmem((2, CANDS // 2, DIM), BF16),
            vmem((2, CANDS, DIM), BF16),
            vmem((4, DIM, PAIR), F32),
            vmem((4, DIM, ROWS), BF16),
            vmem((4, DIM, ROWS), BF16),
            vmem((3, DIM, ROWS), BF16),
            vmem((2, DIM // 2, ROWS), BF16),
            vmem((2, DIM, ROWS), BF16),
            vmem((4, NEGS, DIM), F32),
            vmem((SLOTS, 4 * NEGS), BF16),
            pltpu.SemaphoreType.DMA((3,)),
            pltpu.SemaphoreType.DMA((64,)),
            pltpu.SemaphoreType.DMA((64,)),
        ],
        compiler_params=pltpu.CompilerParams(
            collective_id=0, has_side_effects=True, vmem_limit_bytes=60 * 2**20
        ),
        cost_estimate=pl.CostEstimate(flops=10 * 2**30, bytes_accessed=4 * 2**20, transcendentals=12 * 2**20),
    )(queries, pos_emb, neg_emb, cmeta, qmeta, ymeta)
    return query_grad_t.T * SCALE, item_grad * SCALE, table_grad * SCALE


def solution(mesh):
    rows = P(("group", "batch"), None)
    flat = P(("group", "batch"))
    in_specs = (rows, rows, flat, flat, flat, rows, flat, flat, flat, flat)
    return jax.shard_map(local, mesh=mesh, in_specs=in_specs, out_specs=(rows, rows, rows), check_vma=False)
```

```python
import math

import jax
import jax.numpy as jnp
from jax import lax
from jax.experimental import pallas as pl
from jax.experimental.pallas import tpu as pltpu
from jax.sharding import PartitionSpec as P

MESH = pl.DeviceIdType.MESH
F32 = jnp.float32
BF16 = jnp.bfloat16
LOG2E = math.log2(math.e)
SCALE = 0.125
FLOOR = -1e30

ROWS = 384
NEGS = 128
CANDS = ROWS + NEGS
PAIR = 2 * ROWS
DIM = 256
SLOTS = 512
CHUNK = 32

DIST = (0, 1, 3, 2)
PLACE = (0, 1, 3, 2)


def tiled(x, count):
    return jnp.concatenate([x] * count, axis=1)


def kernel(
    q_in, pos_in, pos_logq_in, pos_ids_in, weight_in, neg_in, neg_logq_in, neg_ids_in, owner_in, slot_in,
    quer_out, item_out, table_out,
    cands, cands_t, quers, scores, raw_a, raw_b, terms, neg_weights, weights_a, weights_b,
    pos_logq, pos_ids, weight, neg_logq, neg_ids, neg_owner, neg_slot,
    cmeta, qmeta, ymeta, logq_col, id_col, stat, decay, stats, shift,
    neg_part, neg_send, neg_got, item_part, item_send, item_relay, item_got,
    quer_part, sib_send, sib_got, quer_send, quer_got,
    neg_rows, onehot, local_sem, send_sem, recv_sem,
):
    g = lax.axis_index("group")
    b = lax.axis_index("batch")
    z, x, c = b // 8, (b // 2) % 4, b % 2
    my_abs = x * 2 + c

    def along_z(step):
        return {"batch": ((z + step) % 4) * 8 + x * 2 + c}

    def along_x(step, flip=0):
        core = (1 - c) if flip else c
        return {"batch": z * 8 + ((x + step) % 4) * 2 + core}

    def along_y(step):
        return {"group": (g + step) % 4}

    sems = iter(range(80))
    sent = []

    def remote(src, dst, target, k=None):
        k = next(sems) if k is None else k
        return pltpu.make_async_remote_copy(
            src_ref=src, dst_ref=dst, send_sem=send_sem.at[k], recv_sem=recv_sem.at[k],
            device_id=target, device_id_type=MESH,
        )

    def go(copy):
        copy.start()
        sent.append(copy)

    peers = [along_z(s) for s in (1, 2, 3)]
    peers += [along_x(s, f) for s in range(4) for f in range(2) if (s, f) != (0, 0)]
    peers += [along_y(s) for s in (1, 2, 3)]
    barrier = pltpu.get_barrier_semaphore()
    for peer in peers:
        pl.semaphore_signal(barrier, inc=1, device_id=peer, device_id_type=MESH)

    pairs = [
        (q_in, quers.at[0, pl.ds(0, ROWS)]),
        (pos_in, cands.at[0, pl.ds(0, ROWS)]),
        (neg_in, cands.at[0, pl.ds(ROWS, NEGS)]),
        (pos_logq_in, pos_logq), (pos_ids_in, pos_ids), (weight_in, weight),
        (neg_logq_in, neg_logq), (neg_ids_in, neg_ids), (owner_in, neg_owner), (slot_in, neg_slot),
    ]
    locals_ = [pltpu.make_async_copy(src, dst, local_sem.at[k]) for k, (src, dst) in enumerate(pairs)]
    for copy in locals_:
        copy.start()
    for copy in locals_:
        copy.wait()
    cmeta[0, 0:1, 0:ROWS] = pos_logq[...].astype(F32).reshape(1, ROWS) * LOG2E
    cmeta[0, 0:1, ROWS:CANDS] = neg_logq[...].astype(F32).reshape(1, NEGS) * LOG2E
    cmeta[0, 1:2, 0:ROWS] = pos_ids[...].reshape(1, ROWS).astype(F32)
    cmeta[0, 1:2, ROWS:CANDS] = neg_ids[...].reshape(1, NEGS).astype(F32)
    qmeta[0, 0:1, 0:ROWS] = pos_ids[...].reshape(1, ROWS).astype(F32)
    qmeta[0, 1:2, 0:ROWS] = weight[...].reshape(1, ROWS)
    ymeta[0] = neg_owner[...].reshape(1, NEGS) * SLOTS + neg_slot[...].reshape(1, NEGS)

    def columns(p):
        cands_t[p] = cands[p].T
        for k in range(CANDS // 128):
            lanes = pl.ds(k * 128, 128)
            for row, ref in ((0, logq_col), (1, id_col)):
                ref[p, lanes, :] = jnp.broadcast_to(cmeta[p, row : row + 1, lanes], (128, 128)).T

    columns(0)
    stat[...] = jnp.concatenate(
        [jnp.full((4, 1, PAIR), FLOOR, F32), jnp.zeros((4, 1, PAIR), F32)], axis=0
    )
    quer_part[...] = jnp.zeros_like(quer_part)
    pl.semaphore_wait(barrier, len(peers))

    qh, ch = ROWS // 2, CANDS // 2

    def quer_at(p, half):
        return quers.at[p, pl.ds(half * qh, qh)]

    def cand_at(p, half):
        return cands.at[p, pl.ds(half * ch, ch)]

    sib = [
        remote(quers.at[p, pl.ds(0, ROWS)], quers.at[p, pl.ds(ROWS, ROWS)], along_x(0, 1)) for p in range(4)
    ]
    quer_up = [remote(quer_at(0, h), quer_at(1, h), along_x(1)) for h in (0, 1)]
    quer_down = [remote(quer_at(0, h), quer_at(2, h), along_x(-1)) for h in (0, 1)]
    quer_far = [
        remote(quer_at(1, 0), quer_at(3, 0), along_x(1)),
        remote(quer_at(2, 1), quer_at(3, 1), along_x(-1)),
    ]
    cand_up = [remote(cand_at(0, h), cand_at(1, h), along_z(1)) for h in (0, 1)]
    cand_down = [remote(cand_at(0, h), cand_at(2, h), along_z(-1)) for h in (0, 1)]
    cand_far = [
        remote(cand_at(1, 0), cand_at(3, 0), along_z(1)),
        remote(cand_at(2, 1), cand_at(3, 1), along_z(-1)),
    ]
    qmeta_copies = {}
    for s in range(4):
        for f in range(2):
            if (s, f) != (0, 0):
                place = qmeta.at[PLACE[s], :, pl.ds(f * ROWS, ROWS)]
                qmeta_copies[(PLACE[s], f)] = remote(qmeta.at[0, :, pl.ds(0, ROWS)], place, along_x(s, f))
    cmeta_copies = {PLACE[s]: remote(cmeta.at[0], cmeta.at[PLACE[s]], along_z(s)) for s in (1, 2, 3)}
    ymeta_copies = [remote(ymeta.at[0], ymeta.at[s], along_y(s)) for s in (1, 2, 3)]
    go(cand_up[0])
    go(cand_down[1])
    go(quer_up[0])
    go(quer_down[1])
    go(sib[0])
    go(qmeta_copies[(0, 1)])
    go(cand_up[1])
    go(cand_down[0])
    go(quer_up[1])
    go(quer_down[0])
    for key, copy in qmeta_copies.items():
        if key != (0, 1):
            go(copy)
    for copy in (*cmeta_copies.values(), *ymeta_copies):
        go(copy)

    def on_target(r):
        r_index = lax.broadcasted_iota(jnp.int32, (CHUNK, PAIR), 0) + r * CHUNK
        q_index = lax.broadcasted_iota(jnp.int32, (CHUNK, PAIR), 1)
        return jnp.logical_and(r_index == q_index, q_index < ROWS)

    def fold(p, cs):
        quer_part[p] = quer_part[p] * decay[...] + jnp.dot(
            cands_t[cs], terms[...], preferred_element_type=F32
        )

    def score(raw, p, cs):
        raw[...] = lax.dot_general(
            cands[cs], quers[p], (((1,), (1,)), ((), ())), preferred_element_type=F32
        )

    def expand(raw, p, cs, diagonal=False):
        row_ids = qmeta[p, 0:1, :]

        def mask(r, peak):
            rows = pl.ds(pl.multiple_of(r * CHUNK, CHUNK), CHUNK)
            s = raw[rows, :] * (SCALE * LOG2E) - tiled(logq_col[cs, rows, :], PAIR // 128)
            drop = tiled(id_col[cs, rows, :], PAIR // 128) == row_ids
            if diagonal:
                drop = jnp.logical_and(drop, jnp.logical_not(on_target(r)))
            s = jnp.where(drop, FLOOR, s)
            scores[p, cs, rows, :] = s
            return jnp.maximum(peak, jnp.max(s.reshape(CHUNK // 8, 8, PAIR), axis=0))

        peak = lax.fori_loop(0, CANDS // CHUNK, mask, jnp.full((8, PAIR), FLOOR, F32), unroll=True)
        old = stat[p]
        new = jnp.maximum(old, jnp.max(peak, axis=0, keepdims=True))

        def add(r, total):
            rows = pl.ds(pl.multiple_of(r * CHUNK, CHUNK), CHUNK)
            e = jnp.exp2(scores[p, cs, rows, :] - new)
            terms[rows, :] = e.astype(BF16)
            return total + jnp.sum(e.reshape(CHUNK // 8, 8, PAIR), axis=0)

        total = lax.fori_loop(0, CANDS // CHUNK, add, jnp.zeros((8, PAIR), F32), unroll=True)
        drop_to = jnp.exp2(old - new)
        decay[...] = drop_to
        stat[p] = new
        stat[4 + p] = stat[4 + p] * drop_to + jnp.sum(total, axis=0, keepdims=True)

    def block(t):
        p = jnp.where(t < 3, t, jnp.where(t < 9, t % 3, jnp.where(t < 12, 3, t - 12)))
        cs = jnp.where(t < 3, 0, jnp.where(t < 9, t // 3, jnp.where(t < 12, t - 9, 3)))
        return p, cs

    def arrived(t, at, do):
        @pl.when(t == at)
        def _():
            do()

    def candidates_from(p, copies):
        def do():
            for copy in (*copies, cmeta_copies[p]):
                copy.wait_recv()
            columns(p)
            if p == 2:
                quer_far[0].wait_recv()
                quer_far[1].wait_recv()
                sib[3].start()

        return do

    def queries_from(p):
        def do():
            sib[p].wait_recv()
            for f in (0, 1):
                qmeta_copies[(p, f)].wait_recv()

        return do

    sib[0].wait_recv()
    qmeta_copies[(0, 1)].wait_recv()
    score(raw_a, 0, 0)
    expand(raw_a, 0, 0, True)
    quer_up[0].wait_recv()
    go(quer_far[0])
    quer_down[1].wait_recv()
    go(quer_far[1])
    cand_up[0].wait_recv()
    go(cand_far[0])
    cand_down[1].wait_recv()
    go(cand_far[1])
    quer_up[1].wait_recv()
    go(sib[1])
    quer_down[0].wait_recv()
    go(sib[2])
    queries_from(1)()
    score(raw_b, 1, 0)

    @pl.loop(0, 7)
    def _(i):
        t = 2 * i + 1
        arrived(t, 1, queries_from(2))
        arrived(t, 5, candidates_from(2, (cand_down[0],)))
        arrived(t, 11, candidates_from(3, cand_far))
        score(raw_a, *block(t + 1))
        fold(*block(t - 1))
        expand(raw_b, *block(t))
        arrived(t, 1, candidates_from(1, (cand_up[1],)))
        arrived(t, 7, queries_from(3))
        score(raw_b, *block(t + 2))
        fold(*block(t))
        expand(raw_a, *block(t + 1))

    sent.append(sib[3])
    fold(*block(14))
    expand(raw_b, *block(15))

    def owner(p, f):
        core = (1 - c) if f else c
        return ((x + 4 - DIST[p]) % 4) * 2 + core

    for p in range(4):
        part = stat[p] + jnp.log(stat[4 + p]) * LOG2E
        for f in range(2):
            stats[my_abs, pl.ds(owner(p, f), 1), :] = part[:, f * ROWS : (f + 1) * ROWS]
    stat_copies = []
    for s in (2, 1, 3, 0):
        for f in range(2):
            if (s, f) != (0, 0):
                j = next(sems)
                go(remote(stats.at[my_abs], stats.at[my_abs], along_x(s, f), j))
                k = owner(PLACE[s], f)
                stat_copies.append(remote(stats.at[k], stats.at[k], along_x(s, f), j))
    fold(*block(15))
    for copy in ymeta_copies:
        copy.wait_recv()
    for k in range(4):
        want = lax.broadcasted_iota(jnp.int32, (SLOTS, NEGS), 0) + g * SLOTS
        onehot[:, k * NEGS : (k + 1) * NEGS] = jnp.where(ymeta[k] == want, 1.0, 0.0).astype(BF16)
    for copy in stat_copies:
        copy.wait_recv()
    peak = stats[0]
    for k in range(1, 8):
        peak = jnp.maximum(peak, stats[k])
    total = jnp.zeros_like(peak)
    for k in range(8):
        total = total + jnp.exp2(stats[k] - peak)
    shift[...] = peak + jnp.log(total) * LOG2E
    lifts, factors = [], []
    for p in range(4):
        lse = jnp.concatenate([shift[pl.ds(owner(p, f), 1), :] for f in range(2)], axis=1)
        lifts.append(jnp.log(qmeta[p, 1:2, :]) * LOG2E - lse)
        factors.append(qmeta[p, 1:2, :] * jnp.exp2(stat[p] - lse))

    sib_parts = [remote(sib_send.at[p], sib_got.at[p], along_x(0, 1)) for p in range(4)]
    for p in (3, 1, 2, 0):
        sib_send[p] = (quer_part[p, :, ROWS:PAIR] * factors[p][:, ROWS:PAIR]).astype(BF16)
        go(sib_parts[p])

    def weigh(cs, r, out, place):
        rows = pl.ds(pl.multiple_of(r * CHUNK, CHUNK), CHUNK)
        for p in range(4):
            gw = jnp.exp2(scores[p, cs, rows, :] + lifts[p])
            if p == 0 and cs == 0:
                gw = jnp.where(on_target(r), gw - qmeta[0, 1:2, :], gw)
            out[place, p * PAIR : (p + 1) * PAIR] = gw.astype(BF16)

    all_quers = quers[...].reshape(4 * PAIR, DIM)

    def weigh_items(cs, out):
        def do(r, carry):
            weigh(cs, r, out, pl.ds(pl.multiple_of(r * CHUNK, CHUNK), CHUNK))
            return carry

        lax.fori_loop(0, ROWS // CHUNK, do, 0, unroll=True)

    for cs in range(4):
        for r in range(NEGS // CHUNK):
            weigh(cs, ROWS // CHUNK + r, neg_weights, pl.ds(cs * NEGS + r * CHUNK, CHUNK))
    neg_part[...] = jnp.dot(neg_weights[...], all_quers, preferred_element_type=F32).reshape(4, NEGS, DIM)
    weigh_items(3, weights_a)
    neg_copies = []
    for p, step in ((3, 2), (1, -1), (2, 1)):
        neg_send[p - 1] = neg_part[p].astype(BF16)
        copy = remote(neg_send.at[p - 1], neg_got.at[p - 1], along_z(step))
        go(copy)
        neg_copies.append(copy)

    def item_block(cs, held, after=None, out=None):
        item_part[cs] = jnp.dot(held[...], all_quers, preferred_element_type=F32)
        if out is not None:
            weigh_items(after, out)

    def summed(p):
        return quer_part[p, :, 0:ROWS] * factors[p][:, 0:ROWS] + sib_got[p].astype(F32)

    quer_copies = []
    for p, step in ((3, 2), (1, -1), (2, 1)):
        sib_parts[p].wait_recv()
        quer_send[p - 1] = summed(p).astype(BF16)
        copy = remote(quer_send.at[p - 1], quer_got.at[p - 1], along_x(step))
        go(copy)
        quer_copies.append(copy)

    ih = ROWS // 2
    up, low = pl.ds(0, ih), pl.ds(ih, ih)
    relay_copies = [
        remote(item_send.at[2, up], item_relay.at[0], along_z(-1)),
        remote(item_send.at[2, low], item_relay.at[1], along_z(1)),
    ]
    to_down = [remote(item_send.at[0, h], item_got.at[0, h], along_z(-1)) for h in (up, low)]
    to_up = [remote(item_send.at[1, h], item_got.at[1, h], along_z(1)) for h in (up, low)]
    item_block(3, weights_a, 1, weights_b)
    item_send[2] = item_part[3].astype(BF16)
    go(relay_copies[1])
    go(relay_copies[0])
    item_block(1, weights_b, 2, weights_a)
    item_send[0, low, :] = item_part[1, low, :].astype(BF16)
    go(to_down[1])
    item_block(2, weights_a, 0, weights_b)
    item_send[1, up, :] = item_part[2, up, :].astype(BF16)
    go(to_up[0])
    item_block(0, weights_b)
    for copy in neg_copies:
        copy.wait_recv()
    neg_rows[0] = (
        neg_part[0] + neg_got[0].astype(F32) + neg_got[1].astype(F32) + neg_got[2].astype(F32)
    ).astype(BF16)
    y_copies = [remote(neg_rows.at[0], neg_rows.at[s], along_y(s)) for s in (2, 1, 3)]
    for copy in y_copies:
        go(copy)
    relay_copies[1].wait_recv()
    item_send[1, low, :] = (item_part[2, low, :] + item_relay[1].astype(F32)).astype(BF16)
    go(to_up[1])
    relay_copies[0].wait_recv()
    item_send[0, up, :] = (item_part[1, up, :] + item_relay[0].astype(F32)).astype(BF16)
    go(to_down[0])

    sib_parts[0].wait_recv()
    own = summed(0) - cands_t[0, :, 0:ROWS].astype(F32) * qmeta[0, 1:2, 0:ROWS]
    for copy in quer_copies:
        copy.wait_recv()
    own = own + quer_got[0].astype(F32) + quer_got[1].astype(F32) + quer_got[2].astype(F32)
    quer_out[...] = (own * SCALE).T
    for copy in y_copies:
        copy.wait_recv()
    table_out[...] = SCALE * jnp.dot(
        onehot[...], neg_rows[...].reshape(4 * NEGS, DIM), preferred_element_type=F32
    )
    for copy in (*to_down, *to_up):
        copy.wait_recv()
    item_out[...] = SCALE * (item_part[0] + item_got[0].astype(F32) + item_got[1].astype(F32))
    for copy in sent:
        copy.wait_send()


def copy_kernel(*refs):
    sems = refs[-1]
    copies = [pltpu.make_async_copy(refs[k], refs[3 + k], sems.at[k]) for k in range(3)]
    for copy in copies:
        copy.start()
    for copy in copies:
        copy.wait()


def local(*args):
    far = pl.BlockSpec(memory_space=pl.ANY)
    here = pl.BlockSpec(memory_space=pltpu.VMEM)
    vmem = pltpu.VMEM
    out_shape = [
        jax.ShapeDtypeStruct((ROWS, DIM), F32),
        jax.ShapeDtypeStruct((ROWS, DIM), F32),
        jax.ShapeDtypeStruct((SLOTS, DIM), F32),
    ]
    results = pl.pallas_call(
        kernel,
        out_shape=[pltpu.VMEM(o.shape, o.dtype) for o in out_shape],
        in_specs=[far] * 10,
        out_specs=[here] * 3,
        scratch_shapes=[
            vmem((4, CANDS, DIM), BF16),
            vmem((4, DIM, CANDS), BF16),
            vmem((4, PAIR, DIM), BF16),
            vmem((4, 4, CANDS, PAIR), F32),
            vmem((CANDS, PAIR), F32),
            vmem((CANDS, PAIR), F32),
            vmem((CANDS, PAIR), BF16),
            vmem((4 * NEGS, 4 * PAIR), BF16),
            vmem((ROWS, 4 * PAIR), BF16),
            vmem((ROWS, 4 * PAIR), BF16),
            vmem((ROWS,), BF16), vmem((ROWS,), jnp.int32), vmem((ROWS,), F32),
            vmem((NEGS,), BF16), vmem((NEGS,), jnp.int32), vmem((NEGS,), jnp.int32), vmem((NEGS,), jnp.int32),
            vmem((4, 2, CANDS), F32),
            vmem((4, 2, PAIR), F32),
            vmem((4, 1, NEGS), jnp.int32),
            vmem((4, CANDS, 128), F32),
            vmem((4, CANDS, 128), F32),
            vmem((8, 1, PAIR), F32),
            vmem((1, PAIR), F32),
            vmem((8, 8, ROWS), F32),
            vmem((8, ROWS), F32),
            vmem((4, NEGS, DIM), F32),
            vmem((3, NEGS, DIM), BF16),
            vmem((3, NEGS, DIM), BF16),
            vmem((4, ROWS, DIM), F32),
            vmem((3, ROWS, DIM), BF16),
            vmem((2, ROWS // 2, DIM), BF16),
            vmem((2, ROWS, DIM), BF16),
            vmem((4, DIM, PAIR), F32),
            vmem((4, DIM, ROWS), BF16),
            vmem((4, DIM, ROWS), BF16),
            vmem((3, DIM, ROWS), BF16),
            vmem((3, DIM, ROWS), BF16),
            vmem((4, NEGS, DIM), BF16),
            vmem((SLOTS, 4 * NEGS), BF16),
            pltpu.SemaphoreType.DMA((10,)),
            pltpu.SemaphoreType.DMA((80,)),
            pltpu.SemaphoreType.DMA((80,)),
        ],
        compiler_params=pltpu.CompilerParams(
            collective_id=0, has_side_effects=True, vmem_limit_bytes=54 * 2**20
        ),
        cost_estimate=pl.CostEstimate(flops=10 * 2**30, bytes_accessed=4 * 2**20, transcendentals=12 * 2**20),
    )(*args)
    return pl.pallas_call(
        copy_kernel,
        out_shape=out_shape,
        in_specs=[here] * 3,
        out_specs=[far] * 3,
        scratch_shapes=[pltpu.SemaphoreType.DMA((3,))],
        compiler_params=pltpu.CompilerParams(vmem_limit_bytes=2**20),
    )(*results)


def solution(mesh):
    rows = P(("group", "batch"), None)
    flat = P(("group", "batch"))
    in_specs = (rows, rows, flat, flat, flat, rows, flat, flat, flat, flat)
    return jax.shard_map(local, mesh=mesh, in_specs=in_specs, out_specs=(rows, rows, rows), check_vma=False)
```

```python
import math

import jax
import jax.numpy as jnp
from jax import lax
from jax.experimental import pallas as pl
from jax.experimental.pallas import tpu as pltpu
from jax.sharding import PartitionSpec as P

MESH = pl.DeviceIdType.MESH
F32 = jnp.float32
BF16 = jnp.bfloat16
LOG2E = math.log2(math.e)
SCALE = 0.125
FLOOR = -1e30

ROWS = 384
NEGS = 128
CANDS = ROWS + NEGS
PAIR = 2 * ROWS
DIM = 256
SLOTS = 512
CHUNK = 32
TALL = DIM + 16
WIDE = PAIR

DIST = (0, 1, 3, 2)
PLACE = (0, 1, 3, 2)


def tiled(x, count):
    return jnp.concatenate([x] * count, axis=1)


def kernel(
    q_in, pos_in, pos_logq_in, pos_ids_in, weight_in, neg_in, neg_logq_in, neg_ids_in, owner_in, slot_in,
    quer_out, item_out, table_out,
    cands, cands_t, quers, scores, raw_a, raw_b, terms, neg_weights, weights_a, weights_b,
    pos_logq, pos_ids, weight, neg_logq, neg_ids, neg_owner, neg_slot,
    cmeta, qmeta, ymeta, logq_col, id_col, stat, decay, stats, shift,
    neg_part, neg_send, neg_got, item_part, item_send, item_relay, item_got,
    quer_part, sib_send, sib_got, quer_send, quer_got,
    neg_rows, onehot, local_sem, send_sem, recv_sem,
):
    g = lax.axis_index("group")
    b = lax.axis_index("batch")
    z, x, c = b // 8, (b // 2) % 4, b % 2
    my_abs = x * 2 + c

    def along_z(step):
        return {"batch": ((z + step) % 4) * 8 + x * 2 + c}

    def along_x(step, flip=0):
        core = (1 - c) if flip else c
        return {"batch": z * 8 + ((x + step) % 4) * 2 + core}

    def along_y(step):
        return {"group": (g + step) % 4}

    sems = iter(range(80))
    sent = []

    def remote(src, dst, target, k=None):
        k = next(sems) if k is None else k
        return pltpu.make_async_remote_copy(
            src_ref=src, dst_ref=dst, send_sem=send_sem.at[k], recv_sem=recv_sem.at[k],
            device_id=target, device_id_type=MESH,
        )

    def go(copy):
        copy.start()
        sent.append(copy)

    peers = [along_z(s) for s in (1, 2, 3)]
    peers += [along_x(s, f) for s in range(4) for f in range(2) if (s, f) != (0, 0)]
    peers += [along_y(s) for s in (1, 2, 3)]
    barrier = pltpu.get_barrier_semaphore()
    for peer in peers:
        pl.semaphore_signal(barrier, inc=1, device_id=peer, device_id_type=MESH)

    pairs = [
        (q_in, quers.at[0, pl.ds(0, ROWS)]),
        (pos_in, cands.at[0, pl.ds(0, ROWS)]),
        (neg_in, cands.at[0, pl.ds(ROWS, NEGS)]),
        (pos_logq_in, pos_logq), (pos_ids_in, pos_ids), (weight_in, weight),
        (neg_logq_in, neg_logq), (neg_ids_in, neg_ids), (owner_in, neg_owner), (slot_in, neg_slot),
    ]
    locals_ = [pltpu.make_async_copy(src, dst, local_sem.at[k]) for k, (src, dst) in enumerate(pairs)]
    for copy in locals_:
        copy.start()
    for copy in locals_[:3]:
        copy.wait()
    pl.semaphore_wait(barrier, len(peers))
    qh, ch = ROWS // 2, CANDS // 2

    def quer_at(p, half):
        return quers.at[p, pl.ds(half * qh, qh)]

    def cand_at(p, half):
        return cands.at[p, pl.ds(half * ch, ch)]

    sib = [
        remote(quers.at[p, pl.ds(0, ROWS)], quers.at[p, pl.ds(ROWS, ROWS)], along_x(0, 1)) for p in range(4)
    ]
    own_quers = quers.at[0, pl.ds(0, ROWS)]
    quer_up = remote(own_quers, quers.at[1, pl.ds(0, ROWS)], along_x(1))
    quer_down = remote(own_quers, quers.at[2, pl.ds(0, ROWS)], along_x(-1))
    quer_far = [
        remote(quer_at(1, 0), quer_at(3, 0), along_x(1)),
        remote(quer_at(2, 1), quer_at(3, 1), along_x(-1)),
    ]
    cand_up = remote(cands.at[0], cands.at[1], along_z(1))
    cand_down = remote(cands.at[0], cands.at[2], along_z(-1))
    cand_far = [
        remote(cand_at(1, 0), cand_at(3, 0), along_z(1)),
        remote(cand_at(2, 1), cand_at(3, 1), along_z(-1)),
    ]
    go(cand_up)
    go(cand_down)
    go(quer_up)
    go(quer_down)
    go(sib[0])
    for copy in locals_[3:]:
        copy.wait()
    cmeta[0, 0:1, 0:ROWS] = pos_logq[...].astype(F32).reshape(1, ROWS) * LOG2E
    cmeta[0, 0:1, ROWS:CANDS] = neg_logq[...].astype(F32).reshape(1, NEGS) * LOG2E
    cmeta[0, 1:2, 0:ROWS] = pos_ids[...].reshape(1, ROWS).astype(F32)
    cmeta[0, 1:2, ROWS:CANDS] = neg_ids[...].reshape(1, NEGS).astype(F32)
    qmeta[0, 0:1, 0:ROWS] = pos_ids[...].reshape(1, ROWS).astype(F32)
    qmeta[0, 1:2, 0:ROWS] = weight[...].reshape(1, ROWS)
    ymeta[0] = neg_owner[...].reshape(1, NEGS) * SLOTS + neg_slot[...].reshape(1, NEGS)

    def columns(p):
        cands_t[p, 0:DIM, :] = cands[p].T
        for k in range(CANDS // 128):
            lanes = pl.ds(k * 128, 128)
            for row, ref in ((0, logq_col), (1, id_col)):
                ref[p, lanes, :] = jnp.broadcast_to(cmeta[p, row : row + 1, lanes], (128, 128)).T


    qmeta_copies = {}
    for s in range(4):
        for f in range(2):
            if (s, f) != (0, 0):
                place = qmeta.at[PLACE[s], :, pl.ds(f * ROWS, ROWS)]
                qmeta_copies[(PLACE[s], f)] = remote(qmeta.at[0, :, pl.ds(0, ROWS)], place, along_x(s, f))
    cmeta_copies = {PLACE[s]: remote(cmeta.at[0], cmeta.at[PLACE[s]], along_z(s)) for s in (1, 2, 3)}
    ymeta_copies = [remote(ymeta.at[0], ymeta.at[s], along_y(s)) for s in (1, 2, 3)]
    go(qmeta_copies[(0, 1)])
    for key, copy in qmeta_copies.items():
        if key != (0, 1):
            go(copy)
    for copy in (*cmeta_copies.values(), *ymeta_copies):
        go(copy)

    columns(0)
    stat[...] = jnp.full((4, 1, PAIR), FLOOR, F32)
    cands_t[:, DIM:TALL, :] = jnp.ones((4, TALL - DIM, CANDS), BF16)
    quer_part[...] = jnp.zeros_like(quer_part)

    def on_target(r, first=0, width=PAIR):
        r_index = lax.broadcasted_iota(jnp.int32, (CHUNK, width), 0) + r * CHUNK
        q_index = lax.broadcasted_iota(jnp.int32, (CHUNK, width), 1) + first
        return jnp.logical_and(r_index == q_index, q_index < ROWS)

    def score(raw, p, cs, n):
        raw[:, n : n + WIDE] = lax.dot_general(
            cands[cs], quers[p, n : n + WIDE, :], (((1,), (1,)), ((), ())), preferred_element_type=F32
        )

    def fold(p, cs, n):
        quer_part[p, :, n : n + WIDE] = quer_part[p, :, n : n + WIDE] * decay[:, n : n + WIDE] + jnp.dot(
            cands_t[cs], terms[:, n : n + WIDE], preferred_element_type=F32
        )

    def expand(raw, p, cs, n, diagonal=False):
        lanes = slice(n, n + WIDE)
        row_ids = qmeta[p, 0:1, lanes]

        def mask(r, peak):
            rows = pl.ds(pl.multiple_of(r * CHUNK, CHUNK), CHUNK)
            s = raw[rows, lanes] * (SCALE * LOG2E) - tiled(logq_col[cs, rows, :], WIDE // 128)
            drop = tiled(id_col[cs, rows, :], WIDE // 128) == row_ids
            if diagonal:
                drop = jnp.logical_and(drop, jnp.logical_not(on_target(r, n, WIDE)))
            s = jnp.where(drop, FLOOR, s)
            scores[p, cs, rows, lanes] = s
            return jnp.maximum(peak, jnp.max(s.reshape(CHUNK // 8, 8, WIDE), axis=0))

        peak = lax.fori_loop(0, CANDS // CHUNK, mask, jnp.full((8, WIDE), FLOOR, F32), unroll=True)
        old = stat[p, :, lanes]
        new = jnp.maximum(old, jnp.max(peak, axis=0, keepdims=True))

        def add(r, carry):
            rows = pl.ds(pl.multiple_of(r * CHUNK, CHUNK), CHUNK)
            terms[rows, lanes] = jnp.exp2(scores[p, cs, rows, lanes] - new).astype(BF16)
            return carry

        lax.fori_loop(0, CANDS // CHUNK, add, 0, unroll=True)
        decay[:, lanes] = jnp.exp2(old - new)
        stat[p, :, lanes] = new

    def step(now, raw, ahead=None, raw_ahead=None, before=None, diagonal=False):
        for n in range(0, PAIR, WIDE):
            if ahead is not None:
                score(raw_ahead, *ahead, n)
            if before is not None:
                fold(*before, n)
            expand(raw, *now, n, diagonal)

    order = [(p, 0) for p in range(3)] + [(p, cs) for cs in (1, 2) for p in range(3)]
    order += [(3, cs) for cs in range(3)] + [(p, 3) for p in range(4)]

    def candidates_from(p, copies):
        for copy in (*copies, cmeta_copies[p]):
            copy.wait_recv()
        columns(p)

    def queries_from(p):
        sib[p].wait_recv()
        for f in (0, 1):
            qmeta_copies[(p, f)].wait_recv()

    sib[0].wait_recv()
    qmeta_copies[(0, 1)].wait_recv()
    for n in range(0, PAIR, WIDE):
        score(raw_a, 0, 0, n)
    step((0, 0), raw_a, diagonal=True)
    quer_up.wait_recv()
    go(sib[1])
    quer_down.wait_recv()
    go(sib[2])
    go(quer_far[0])
    go(quer_far[1])
    cand_up.wait_recv()
    go(cand_far[0])
    cand_down.wait_recv()
    go(cand_far[1])
    queries_from(1)
    score(raw_b, 1, 0, 0)
    raws = (raw_a, raw_b)
    for t in range(1, 16):
        ahead = order[t + 1] if t < 15 else None
        if ahead == (2, 0):
            queries_from(2)
        elif ahead == (0, 1):
            candidates_from(1, ())
        elif ahead == (0, 2):
            candidates_from(2, ())
            quer_far[0].wait_recv()
            quer_far[1].wait_recv()
            go(sib[3])
        elif ahead == (3, 0):
            queries_from(3)
        elif ahead == (0, 3):
            candidates_from(3, cand_far)
        step(order[t], raws[t % 2], ahead, raws[(t + 1) % 2], order[t - 1])
    fold(*order[15], 0)

    def owner(p, f):
        core = (1 - c) if f else c
        return ((x + 4 - DIST[p]) % 4) * 2 + core

    def count(p):
        return quer_part[p, DIM : DIM + 1, :]

    for p in range(4):
        part = stat[p] + jnp.log(count(p)) * LOG2E
        for f in range(2):
            stats[my_abs, pl.ds(owner(p, f), 1), :] = part[:, f * ROWS : (f + 1) * ROWS]
    stat_copies = {}
    for s in (2, 1, 3, 0):
        for f in range(2):
            if (s, f) != (0, 0):
                j = next(sems)
                go(remote(stats.at[my_abs], stats.at[my_abs], along_x(s, f), j))
                k = owner(PLACE[s], f)
                stat_copies[(s, f)] = remote(stats.at[k], stats.at[k], along_x(s, f), j)

    sib_parts = [remote(sib_send.at[p], sib_got.at[p], along_x(0, 1)) for p in range(4)]
    for p in (3, 1, 2, 0):
        share = 1.0 / count(p)[:, ROWS:PAIR]
        sib_send[p] = (quer_part[p, 0:DIM, ROWS:PAIR] * share).astype(BF16)
        go(sib_parts[p])
    stat_copies[(0, 1)].wait_recv()

    def chip_average(p):
        row = pl.ds(owner(p, 0), 1)
        mine, other = stats[my_abs, row, :], stats[owner(0, 1), row, :]
        top = jnp.maximum(mine, other)
        mine, other = jnp.exp2(mine - top), jnp.exp2(other - top)
        both = 1.0 / (mine + other)
        mine, other = mine * both / count(p)[:, 0:ROWS], other * both
        return quer_part[p, 0:DIM, 0:ROWS] * mine + sib_got[p].astype(F32) * other

    quer_copies = []
    for p, step_x in ((3, 2), (1, -1), (2, 1)):
        sib_parts[p].wait_recv()
        quer_send[p - 1] = chip_average(p).astype(BF16)
        copy = remote(quer_send.at[p - 1], quer_got.at[p - 1], along_x(step_x))
        go(copy)
        quer_copies.append(copy)
    for copy in ymeta_copies:
        copy.wait_recv()
    for k in range(4):
        want = lax.broadcasted_iota(jnp.int32, (SLOTS, NEGS), 0) + g * SLOTS
        onehot[:, k * NEGS : (k + 1) * NEGS] = jnp.where(ymeta[k] == want, 1.0, 0.0).astype(BF16)
    for key, copy in stat_copies.items():
        if key != (0, 1):
            copy.wait_recv()
    peak = stats[0]
    for k in range(1, 8):
        peak = jnp.maximum(peak, stats[k])
    total = jnp.zeros_like(peak)
    for k in range(8):
        total = total + jnp.exp2(stats[k] - peak)
    shift[...] = peak + jnp.log(total) * LOG2E
    lifts = []
    for p in range(4):
        lse = jnp.concatenate([shift[pl.ds(owner(p, f), 1), :] for f in range(2)], axis=1)
        lifts.append(jnp.log(qmeta[p, 1:2, :]) * LOG2E - lse)

    def weigh(cs, r, out, place):
        rows = pl.ds(pl.multiple_of(r * CHUNK, CHUNK), CHUNK)
        for p in range(4):
            gw = jnp.exp2(scores[p, cs, rows, :] + lifts[p])
            if p == 0 and cs == 0:
                gw = jnp.where(on_target(r), gw - qmeta[0, 1:2, :], gw)
            out[place, p * PAIR : (p + 1) * PAIR] = gw.astype(BF16)

    all_quers = quers[...].reshape(4 * PAIR, DIM)

    def weigh_items(cs, out):
        def do(r, carry):
            weigh(cs, r, out, pl.ds(pl.multiple_of(r * CHUNK, CHUNK), CHUNK))
            return carry

        lax.fori_loop(0, ROWS // CHUNK, do, 0, unroll=True)

    for cs in range(4):
        for r in range(NEGS // CHUNK):
            weigh(cs, ROWS // CHUNK + r, neg_weights, pl.ds(cs * NEGS + r * CHUNK, CHUNK))
    neg_part[...] = jnp.dot(neg_weights[...], all_quers, preferred_element_type=F32).reshape(4, NEGS, DIM)
    weigh_items(3, weights_a)
    neg_copies = []
    for p, step in ((3, 2), (1, -1), (2, 1)):
        neg_send[p - 1] = neg_part[p].astype(BF16)
        copy = remote(neg_send.at[p - 1], neg_got.at[p - 1], along_z(step))
        go(copy)
        neg_copies.append(copy)

    def item_block(cs, held, after=None, out=None):
        item_part[cs] = jnp.dot(held[...], all_quers, preferred_element_type=F32)
        if out is not None:
            weigh_items(after, out)

    ih = ROWS // 2
    up, low = pl.ds(0, ih), pl.ds(ih, ih)
    relay_copies = [
        remote(item_send.at[2, up], item_relay.at[0], along_z(-1)),
        remote(item_send.at[2, low], item_relay.at[1], along_z(1)),
    ]
    to_down = [remote(item_send.at[0, h], item_got.at[0, h], along_z(-1)) for h in (up, low)]
    to_up = [remote(item_send.at[1, h], item_got.at[1, h], along_z(1)) for h in (up, low)]
    item_block(3, weights_a, 1, weights_b)
    item_send[2] = item_part[3].astype(BF16)
    go(relay_copies[1])
    go(relay_copies[0])
    item_block(1, weights_b, 2, weights_a)
    item_send[0, low, :] = item_part[1, low, :].astype(BF16)
    go(to_down[1])
    item_block(2, weights_a, 0, weights_b)
    item_send[1, up, :] = item_part[2, up, :].astype(BF16)
    go(to_up[0])
    item_block(0, weights_b)
    for copy in neg_copies:
        copy.wait_recv()
    neg_rows[0] = (
        neg_part[0] + neg_got[0].astype(F32) + neg_got[1].astype(F32) + neg_got[2].astype(F32)
    ).astype(BF16)
    y_copies = [remote(neg_rows.at[0], neg_rows.at[s], along_y(s)) for s in (2, 1, 3)]
    for copy in y_copies:
        go(copy)
    relay_copies[1].wait_recv()
    item_send[1, low, :] = (item_part[2, low, :] + item_relay[1].astype(F32)).astype(BF16)
    go(to_up[1])
    relay_copies[0].wait_recv()
    item_send[0, up, :] = (item_part[1, up, :] + item_relay[0].astype(F32)).astype(BF16)
    go(to_down[0])

    my_row = pl.ds(my_abs, 1)

    def chip_weight(step):
        k = ((x + step) % 4) * 2
        return sum(jnp.exp2(stats[k + f, my_row, :] - shift[my_row, :]) for f in range(2))

    sib_parts[0].wait_recv()
    own = chip_average(0) * chip_weight(0)
    for k, step_x in ((2, 2), (0, 1), (1, 3)):
        quer_copies[(1, 2, 0)[k]].wait_recv()
        own = own + quer_got[k].astype(F32) * chip_weight(step_x)
    own = (own - cands_t[0, 0:DIM, 0:ROWS].astype(F32)) * qmeta[0, 1:2, 0:ROWS]
    quer_out[...] = (own * SCALE).T
    for copy in y_copies:
        copy.wait_recv()
    table_out[...] = SCALE * jnp.dot(
        onehot[...], neg_rows[...].reshape(4 * NEGS, DIM), preferred_element_type=F32
    )
    for copy in (*to_down, *to_up):
        copy.wait_recv()
    item_out[...] = SCALE * (item_part[0] + item_got[0].astype(F32) + item_got[1].astype(F32))
    for copy in sent:
        copy.wait_send()


def copy_kernel(*refs):
    sems = refs[-1]
    copies = [pltpu.make_async_copy(refs[k], refs[3 + k], sems.at[k]) for k in range(3)]
    for copy in copies:
        copy.start()
    for copy in copies:
        copy.wait()


def local(*args):
    far = pl.BlockSpec(memory_space=pl.ANY)
    here = pl.BlockSpec(memory_space=pltpu.VMEM)
    vmem = pltpu.VMEM
    out_shape = [
        jax.ShapeDtypeStruct((ROWS, DIM), F32),
        jax.ShapeDtypeStruct((ROWS, DIM), F32),
        jax.ShapeDtypeStruct((SLOTS, DIM), F32),
    ]
    results = pl.pallas_call(
        kernel,
        out_shape=[pltpu.VMEM(o.shape, o.dtype) for o in out_shape],
        in_specs=[far] * 10,
        out_specs=[here] * 3,
        scratch_shapes=[
            vmem((4, CANDS, DIM), BF16),
            vmem((4, TALL, CANDS), BF16),
            vmem((4, PAIR, DIM), BF16),
            vmem((4, 4, CANDS, PAIR), F32),
            vmem((CANDS, PAIR), F32),
            vmem((CANDS, PAIR), F32),
            vmem((CANDS, PAIR), BF16),
            vmem((4 * NEGS, 4 * PAIR), BF16),
            vmem((ROWS, 4 * PAIR), BF16),
            vmem((ROWS, 4 * PAIR), BF16),
            vmem((ROWS,), BF16), vmem((ROWS,), jnp.int32), vmem((ROWS,), F32),
            vmem((NEGS,), BF16), vmem((NEGS,), jnp.int32), vmem((NEGS,), jnp.int32), vmem((NEGS,), jnp.int32),
            vmem((4, 2, CANDS), F32),
            vmem((4, 2, PAIR), F32),
            vmem((4, 1, NEGS), jnp.int32),
            vmem((4, CANDS, 128), F32),
            vmem((4, CANDS, 128), F32),
            vmem((4, 1, PAIR), F32),
            vmem((1, PAIR), F32),
            vmem((8, 8, ROWS), F32),
            vmem((8, ROWS), F32),
            vmem((4, NEGS, DIM), F32),
            vmem((3, NEGS, DIM), BF16),
            vmem((3, NEGS, DIM), BF16),
            vmem((4, ROWS, DIM), F32),
            vmem((3, ROWS, DIM), BF16),
            vmem((2, ROWS // 2, DIM), BF16),
            vmem((2, ROWS, DIM), BF16),
            vmem((4, TALL, PAIR), F32),
            vmem((4, DIM, ROWS), BF16),
            vmem((4, DIM, ROWS), BF16),
            vmem((3, DIM, ROWS), BF16),
            vmem((3, DIM, ROWS), BF16),
            vmem((4, NEGS, DIM), BF16),
            vmem((SLOTS, 4 * NEGS), BF16),
            pltpu.SemaphoreType.DMA((10,)),
            pltpu.SemaphoreType.DMA((80,)),
            pltpu.SemaphoreType.DMA((80,)),
        ],
        compiler_params=pltpu.CompilerParams(
            collective_id=0, has_side_effects=True, vmem_limit_bytes=54 * 2**20
        ),
        cost_estimate=pl.CostEstimate(flops=10 * 2**30, bytes_accessed=4 * 2**20, transcendentals=12 * 2**20),
    )(*args)
    return pl.pallas_call(
        copy_kernel,
        out_shape=out_shape,
        in_specs=[here] * 3,
        out_specs=[far] * 3,
        scratch_shapes=[pltpu.SemaphoreType.DMA((3,))],
        compiler_params=pltpu.CompilerParams(vmem_limit_bytes=2**20),
    )(*results)


def solution(mesh):
    rows = P(("group", "batch"), None)
    flat = P(("group", "batch"))
    in_specs = (rows, rows, flat, flat, flat, rows, flat, flat, flat, flat)
    return jax.shard_map(local, mesh=mesh, in_specs=in_specs, out_specs=(rows, rows, rows), check_vma=False)
```

```python
import math

import jax
import jax.numpy as jnp
from jax import lax
from jax.experimental import pallas as pl
from jax.experimental.pallas import tpu as pltpu
from jax.sharding import PartitionSpec as P

MESH = pl.DeviceIdType.MESH
F32 = jnp.float32
BF16 = jnp.bfloat16
LOG2E = math.log2(math.e)
SCALE = 0.125
FLOOR = -1e30

ROWS = 384
NEGS = 128
CANDS = ROWS + NEGS
PAIR = 2 * ROWS
DIM = 256
SLOTS = 512
CHUNK = 32
TALL = DIM + 16
WIDE = PAIR

DIST = (0, 1, 3, 2)
PLACE = (0, 1, 3, 2)


def tiled(x, count):
    return jnp.concatenate([x] * count, axis=1)


def kernel(
    q_in, pos_in, pos_logq_in, pos_ids_in, weight_in, neg_in, neg_logq_in, neg_ids_in, owner_in, slot_in,
    quer_out, item_out, table_out,
    cands, cands_t, quers, scores, raw_a, raw_b, terms, neg_weights, weights_a, weights_b,
    pos_logq, pos_ids, weight, neg_logq, neg_ids, neg_owner, neg_slot,
    cmeta, qmeta, ymeta, logq_col, id_col, stat, decay, stats, shift,
    neg_part, neg_send, neg_got, item_part, item_send, item_relay, item_got,
    quer_part, sib_send, sib_got, quer_send, quer_got,
    neg_rows, onehot, local_sem, send_sem, recv_sem,
):
    g = lax.axis_index("group")
    b = lax.axis_index("batch")
    z, x, c = b // 8, (b // 2) % 4, b % 2
    my_abs = x * 2 + c

    def along_z(step):
        return {"batch": ((z + step) % 4) * 8 + x * 2 + c}

    def along_x(step, flip=0):
        core = (1 - c) if flip else c
        return {"batch": z * 8 + ((x + step) % 4) * 2 + core}

    def along_y(step):
        return {"group": (g + step) % 4}

    sems = iter(range(80))
    sent = []

    def remote(src, dst, target, k=None):
        k = next(sems) if k is None else k
        return pltpu.make_async_remote_copy(
            src_ref=src, dst_ref=dst, send_sem=send_sem.at[k], recv_sem=recv_sem.at[k],
            device_id=target, device_id_type=MESH,
        )

    def go(copy):
        copy.start()
        sent.append(copy)

    peers = [along_z(s) for s in (1, 2, 3)]
    peers += [along_x(s, f) for s in range(4) for f in range(2) if (s, f) != (0, 0)]
    peers += [along_y(s) for s in (1, 2, 3)]
    barrier = pltpu.get_barrier_semaphore()
    for peer in peers:
        pl.semaphore_signal(barrier, inc=1, device_id=peer, device_id_type=MESH)

    pairs = [
        (q_in, quers.at[0, pl.ds(0, ROWS)]),
        (pos_in, cands.at[0, pl.ds(0, ROWS)]),
        (neg_in, cands.at[0, pl.ds(ROWS, NEGS)]),
        (pos_logq_in, pos_logq), (pos_ids_in, pos_ids), (weight_in, weight),
        (neg_logq_in, neg_logq), (neg_ids_in, neg_ids), (owner_in, neg_owner), (slot_in, neg_slot),
    ]
    locals_ = [pltpu.make_async_copy(src, dst, local_sem.at[k]) for k, (src, dst) in enumerate(pairs)]
    for copy in locals_:
        copy.start()
    for copy in locals_[:3]:
        copy.wait()
    pl.semaphore_wait(barrier, len(peers))
    qh, ch = ROWS // 2, CANDS // 2

    def quer_at(p, half):
        return quers.at[p, pl.ds(half * qh, qh)]

    def cand_at(p, half):
        return cands.at[p, pl.ds(half * ch, ch)]

    sib = [
        remote(quers.at[p, pl.ds(0, ROWS)], quers.at[p, pl.ds(ROWS, ROWS)], along_x(0, 1)) for p in range(4)
    ]
    own_quers = quers.at[0, pl.ds(0, ROWS)]
    quer_up = remote(own_quers, quers.at[1, pl.ds(0, ROWS)], along_x(1))
    quer_down = remote(own_quers, quers.at[2, pl.ds(0, ROWS)], along_x(-1))
    quer_far = [
        remote(quer_at(1, 0), quer_at(3, 0), along_x(1)),
        remote(quer_at(2, 1), quer_at(3, 1), along_x(-1)),
    ]
    cand_up = remote(cands.at[0], cands.at[1], along_z(1))
    cand_down = remote(cands.at[0], cands.at[2], along_z(-1))
    cand_far = [
        remote(cand_at(1, 0), cand_at(3, 0), along_z(1)),
        remote(cand_at(2, 1), cand_at(3, 1), along_z(-1)),
    ]
    go(cand_up)
    go(cand_down)
    go(quer_up)
    go(quer_down)
    go(sib[0])
    for copy in locals_[3:]:
        copy.wait()
    cmeta[0, 0:1, 0:ROWS] = pos_logq[...].astype(F32).reshape(1, ROWS) * LOG2E
    cmeta[0, 0:1, ROWS:CANDS] = neg_logq[...].astype(F32).reshape(1, NEGS) * LOG2E
    cmeta[0, 1:2, 0:ROWS] = pos_ids[...].reshape(1, ROWS).astype(F32)
    cmeta[0, 1:2, ROWS:CANDS] = neg_ids[...].reshape(1, NEGS).astype(F32)
    qmeta[0, 0:1, 0:ROWS] = pos_ids[...].reshape(1, ROWS).astype(F32)
    qmeta[0, 1:2, 0:ROWS] = weight[...].reshape(1, ROWS)
    ymeta[0] = neg_owner[...].reshape(1, NEGS) * SLOTS + neg_slot[...].reshape(1, NEGS)

    def columns(p):
        cands_t[p, 0:DIM, :] = cands[p].T
        for k in range(CANDS // 128):
            lanes = pl.ds(k * 128, 128)
            for row, ref in ((0, logq_col), (1, id_col)):
                ref[p, lanes, :] = jnp.broadcast_to(cmeta[p, row : row + 1, lanes], (128, 128)).T


    qmeta_copies = {}
    for s in range(4):
        for f in range(2):
            if (s, f) != (0, 0):
                place = qmeta.at[PLACE[s], :, pl.ds(f * ROWS, ROWS)]
                qmeta_copies[(PLACE[s], f)] = remote(qmeta.at[0, :, pl.ds(0, ROWS)], place, along_x(s, f))
    cmeta_copies = {PLACE[s]: remote(cmeta.at[0], cmeta.at[PLACE[s]], along_z(s)) for s in (1, 2, 3)}
    ymeta_copies = [remote(ymeta.at[0], ymeta.at[s], along_y(s)) for s in (1, 2, 3)]
    go(qmeta_copies[(0, 1)])
    for key, copy in qmeta_copies.items():
        if key != (0, 1):
            go(copy)
    for copy in (*cmeta_copies.values(), *ymeta_copies):
        go(copy)

    columns(0)
    stat[...] = jnp.full((4, 1, PAIR), FLOOR, F32)
    cands_t[:, DIM:TALL, :] = jnp.ones((4, TALL - DIM, CANDS), BF16)
    quer_part[...] = jnp.zeros_like(quer_part)

    def on_target(r, first=0, width=PAIR):
        r_index = lax.broadcasted_iota(jnp.int32, (CHUNK, width), 0) + r * CHUNK
        q_index = lax.broadcasted_iota(jnp.int32, (CHUNK, width), 1) + first
        return jnp.logical_and(r_index == q_index, q_index < ROWS)

    def score(raw, p, cs, n):
        raw[:, n : n + WIDE] = lax.dot_general(
            cands[cs], quers[p, n : n + WIDE, :], (((1,), (1,)), ((), ())), preferred_element_type=F32
        )

    def fold(p, cs, n):
        quer_part[p, :, n : n + WIDE] = quer_part[p, :, n : n + WIDE] * decay[:, n : n + WIDE] + jnp.dot(
            cands_t[cs], terms[:, n : n + WIDE], preferred_element_type=F32
        )

    def expand(raw, p, cs, n, diagonal=False):
        lanes = slice(n, n + WIDE)
        row_ids = qmeta[p, 0:1, lanes]

        def mask(r, peak):
            rows = pl.ds(pl.multiple_of(r * CHUNK, CHUNK), CHUNK)
            s = raw[rows, lanes] * (SCALE * LOG2E) - tiled(logq_col[cs, rows, :], WIDE // 128)
            drop = tiled(id_col[cs, rows, :], WIDE // 128) == row_ids
            if diagonal:
                drop = jnp.logical_and(drop, jnp.logical_not(on_target(r, n, WIDE)))
            s = jnp.where(drop, FLOOR, s)
            scores[p, cs, rows, lanes] = s
            return jnp.maximum(peak, jnp.max(s.reshape(CHUNK // 8, 8, WIDE), axis=0))

        peak = lax.fori_loop(0, CANDS // CHUNK, mask, jnp.full((8, WIDE), FLOOR, F32), unroll=True)
        old = stat[p, :, lanes]
        new = jnp.maximum(old, jnp.max(peak, axis=0, keepdims=True))

        def add(r, carry):
            rows = pl.ds(pl.multiple_of(r * CHUNK, CHUNK), CHUNK)
            terms[rows, lanes] = jnp.exp2(scores[p, cs, rows, lanes] - new).astype(BF16)
            return carry

        lax.fori_loop(0, CANDS // CHUNK, add, 0, unroll=True)
        decay[:, lanes] = jnp.exp2(old - new)
        stat[p, :, lanes] = new

    def step(now, raw, ahead=None, raw_ahead=None, before=None, diagonal=False):
        for n in range(0, PAIR, WIDE):
            if ahead is not None:
                score(raw_ahead, *ahead, n)
            if before is not None:
                fold(*before, n)
            expand(raw, *now, n, diagonal)

    order = [(p, 0) for p in range(3)] + [(p, cs) for cs in (1, 2) for p in range(3)]
    order += [(3, cs) for cs in range(3)] + [(p, 3) for p in range(4)]

    def candidates_from(p, copies):
        for copy in (*copies, cmeta_copies[p]):
            copy.wait_recv()
        columns(p)

    def queries_from(p):
        sib[p].wait_recv()
        for f in (0, 1):
            qmeta_copies[(p, f)].wait_recv()

    sib[0].wait_recv()
    qmeta_copies[(0, 1)].wait_recv()
    for n in range(0, PAIR, WIDE):
        score(raw_a, 0, 0, n)
    step((0, 0), raw_a, diagonal=True)
    quer_up.wait_recv()
    go(sib[1])
    quer_down.wait_recv()
    go(sib[2])
    go(quer_far[0])
    go(quer_far[1])
    cand_up.wait_recv()
    go(cand_far[0])
    cand_down.wait_recv()
    go(cand_far[1])
    queries_from(1)
    score(raw_b, 1, 0, 0)
    raws = (raw_a, raw_b)
    for t in range(1, 16):
        ahead = order[t + 1] if t < 15 else None
        if ahead == (2, 0):
            queries_from(2)
        elif ahead == (0, 1):
            candidates_from(1, ())
        elif ahead == (0, 2):
            candidates_from(2, ())
            quer_far[0].wait_recv()
            quer_far[1].wait_recv()
            go(sib[3])
        elif ahead == (3, 0):
            queries_from(3)
        elif ahead == (0, 3):
            candidates_from(3, cand_far)
        step(order[t], raws[t % 2], ahead, raws[(t + 1) % 2], order[t - 1])
    fold(*order[15], 0)

    def owner(p, f):
        core = (1 - c) if f else c
        return ((x + 4 - DIST[p]) % 4) * 2 + core

    def count(p):
        return quer_part[p, DIM : DIM + 1, :]

    for p in range(4):
        part = stat[p] + jnp.log(count(p)) * LOG2E
        for f in range(2):
            stats[my_abs, pl.ds(owner(p, f), 1), :] = part[:, f * ROWS : (f + 1) * ROWS]
    stat_copies = {}
    for s in (2, 1, 3, 0):
        for f in range(2):
            if (s, f) != (0, 0):
                j = next(sems)
                go(remote(stats.at[my_abs], stats.at[my_abs], along_x(s, f), j))
                k = owner(PLACE[s], f)
                stat_copies[(s, f)] = remote(stats.at[k], stats.at[k], along_x(s, f), j)

    sib_parts = [remote(sib_send.at[p], sib_got.at[p], along_x(0, 1)) for p in range(4)]
    for p in (3, 1, 2, 0):
        share = 1.0 / count(p)[:, ROWS:PAIR]
        sib_send[p] = (quer_part[p, 0:DIM, ROWS:PAIR] * share).astype(BF16)
        go(sib_parts[p])
    stat_copies[(0, 1)].wait_recv()

    def chip_average(p):
        row = pl.ds(owner(p, 0), 1)
        mine, other = stats[my_abs, row, :], stats[owner(0, 1), row, :]
        top = jnp.maximum(mine, other)
        mine, other = jnp.exp2(mine - top), jnp.exp2(other - top)
        both = 1.0 / (mine + other)
        mine, other = mine * both / count(p)[:, 0:ROWS], other * both
        return quer_part[p, 0:DIM, 0:ROWS] * mine + sib_got[p].astype(F32) * other

    quer_copies = []
    for p, step_x in ((3, 2), (1, -1), (2, 1)):
        sib_parts[p].wait_recv()
        quer_send[p - 1] = chip_average(p).astype(BF16)
        copy = remote(quer_send.at[p - 1], quer_got.at[p - 1], along_x(step_x))
        go(copy)
        quer_copies.append(copy)
    for copy in ymeta_copies:
        copy.wait_recv()
    for k in range(4):
        want = lax.broadcasted_iota(jnp.int32, (SLOTS, NEGS), 0) + g * SLOTS
        onehot[:, k * NEGS : (k + 1) * NEGS] = jnp.where(ymeta[k] == want, 1.0, 0.0).astype(BF16)
    for key, copy in stat_copies.items():
        if key != (0, 1):
            copy.wait_recv()
    peak = stats[0]
    for k in range(1, 8):
        peak = jnp.maximum(peak, stats[k])
    total = jnp.zeros_like(peak)
    for k in range(8):
        total = total + jnp.exp2(stats[k] - peak)
    shift[...] = peak + jnp.log(total) * LOG2E
    lifts = []
    for p in range(4):
        lse = jnp.concatenate([shift[pl.ds(owner(p, f), 1), :] for f in range(2)], axis=1)
        lifts.append(jnp.log(qmeta[p, 1:2, :]) * LOG2E - lse)

    def weigh(cs, r, out, place):
        rows = pl.ds(pl.multiple_of(r * CHUNK, CHUNK), CHUNK)
        for p in range(4):
            gw = jnp.exp2(scores[p, cs, rows, :] + lifts[p])
            if p == 0 and cs == 0:
                gw = jnp.where(on_target(r), gw - qmeta[0, 1:2, :], gw)
            out[place, p * PAIR : (p + 1) * PAIR] = gw.astype(BF16)

    all_quers = quers[...].reshape(4 * PAIR, DIM)

    def weigh_items(cs, out):
        def do(r, carry):
            weigh(cs, r, out, pl.ds(pl.multiple_of(r * CHUNK, CHUNK), CHUNK))
            return carry

        lax.fori_loop(0, ROWS // CHUNK, do, 0, unroll=True)

    neg_copies = []
    steps_z = {3: 2, 1: -1, 2: 1}
    for group in ((2, 3), (0, 1)):
        for cs in group:
            for r in range(NEGS // CHUNK):
                weigh(cs, ROWS // CHUNK + r, neg_weights, pl.ds(cs * NEGS + r * CHUNK, CHUNK))
        first, count_rows = min(group), len(group) * NEGS
        neg_part[first : first + len(group)] = jnp.dot(
            neg_weights[first * NEGS : first * NEGS + count_rows, :], all_quers, preferred_element_type=F32
        ).reshape(len(group), NEGS, DIM)
        for cs in group:
            if cs:
                neg_send[cs - 1] = neg_part[cs].astype(BF16)
                copy = remote(neg_send.at[cs - 1], neg_got.at[cs - 1], along_z(steps_z[cs]))
                go(copy)
                neg_copies.append(copy)
    weigh_items(3, weights_a)

    def item_block(cs, held, after=None, out=None):
        item_part[cs] = jnp.dot(held[...], all_quers, preferred_element_type=F32)
        if out is not None:
            weigh_items(after, out)

    ih = ROWS // 2
    up, low = pl.ds(0, ih), pl.ds(ih, ih)
    relay_copies = [
        remote(item_send.at[2, up], item_relay.at[0], along_z(-1)),
        remote(item_send.at[2, low], item_relay.at[1], along_z(1)),
    ]
    to_down = [remote(item_send.at[0, h], item_got.at[0, h], along_z(-1)) for h in (up, low)]
    to_up = [remote(item_send.at[1, h], item_got.at[1, h], along_z(1)) for h in (up, low)]
    item_block(3, weights_a, 1, weights_b)
    item_send[2] = item_part[3].astype(BF16)
    go(relay_copies[1])
    go(relay_copies[0])
    item_block(1, weights_b, 2, weights_a)
    item_send[0, low, :] = item_part[1, low, :].astype(BF16)
    go(to_down[1])
    item_block(2, weights_a, 0, weights_b)
    item_send[1, up, :] = item_part[2, up, :].astype(BF16)
    go(to_up[0])
    item_block(0, weights_b)
    for copy in neg_copies:
        copy.wait_recv()
    neg_rows[0] = (
        neg_part[0] + neg_got[0].astype(F32) + neg_got[1].astype(F32) + neg_got[2].astype(F32)
    ).astype(BF16)
    y_copies = [remote(neg_rows.at[0], neg_rows.at[s], along_y(s)) for s in (2, 1, 3)]
    for copy in y_copies:
        go(copy)
    relay_copies[1].wait_recv()
    item_send[1, low, :] = (item_part[2, low, :] + item_relay[1].astype(F32)).astype(BF16)
    go(to_up[1])
    relay_copies[0].wait_recv()
    item_send[0, up, :] = (item_part[1, up, :] + item_relay[0].astype(F32)).astype(BF16)
    go(to_down[0])

    my_row = pl.ds(my_abs, 1)

    def chip_weight(step):
        k = ((x + step) % 4) * 2
        return sum(jnp.exp2(stats[k + f, my_row, :] - shift[my_row, :]) for f in range(2))

    sib_parts[0].wait_recv()
    own = chip_average(0) * chip_weight(0)
    for k, step_x in ((2, 2), (0, 1), (1, 3)):
        quer_copies[(1, 2, 0)[k]].wait_recv()
        own = own + quer_got[k].astype(F32) * chip_weight(step_x)
    own = (own - cands_t[0, 0:DIM, 0:ROWS].astype(F32)) * qmeta[0, 1:2, 0:ROWS]
    quer_out[...] = (own * SCALE).T
    for copy in y_copies:
        copy.wait_recv()
    table_out[...] = SCALE * jnp.dot(
        onehot[...], neg_rows[...].reshape(4 * NEGS, DIM), preferred_element_type=F32
    )
    for copy in (*to_down, *to_up):
        copy.wait_recv()
    item_out[...] = SCALE * (item_part[0] + item_got[0].astype(F32) + item_got[1].astype(F32))
    for copy in sent:
        copy.wait_send()


def copy_kernel(*refs):
    sems = refs[-1]
    copies = [pltpu.make_async_copy(refs[k], refs[3 + k], sems.at[k]) for k in range(3)]
    for copy in copies:
        copy.start()
    for copy in copies:
        copy.wait()


def local(*args):
    far = pl.BlockSpec(memory_space=pl.ANY)
    here = pl.BlockSpec(memory_space=pltpu.VMEM)
    vmem = pltpu.VMEM
    out_shape = [
        jax.ShapeDtypeStruct((ROWS, DIM), F32),
        jax.ShapeDtypeStruct((ROWS, DIM), F32),
        jax.ShapeDtypeStruct((SLOTS, DIM), F32),
    ]
    results = pl.pallas_call(
        kernel,
        out_shape=[pltpu.VMEM(o.shape, o.dtype) for o in out_shape],
        in_specs=[far] * 10,
        out_specs=[here] * 3,
        scratch_shapes=[
            vmem((4, CANDS, DIM), BF16),
            vmem((4, TALL, CANDS), BF16),
            vmem((4, PAIR, DIM), BF16),
            vmem((4, 4, CANDS, PAIR), F32),
            vmem((CANDS, PAIR), F32),
            vmem((CANDS, PAIR), F32),
            vmem((CANDS, PAIR), BF16),
            vmem((4 * NEGS, 4 * PAIR), BF16),
            vmem((ROWS, 4 * PAIR), BF16),
            vmem((ROWS, 4 * PAIR), BF16),
            vmem((ROWS,), BF16), vmem((ROWS,), jnp.int32), vmem((ROWS,), F32),
            vmem((NEGS,), BF16), vmem((NEGS,), jnp.int32), vmem((NEGS,), jnp.int32), vmem((NEGS,), jnp.int32),
            vmem((4, 2, CANDS), F32),
            vmem((4, 2, PAIR), F32),
            vmem((4, 1, NEGS), jnp.int32),
            vmem((4, CANDS, 128), F32),
            vmem((4, CANDS, 128), F32),
            vmem((4, 1, PAIR), F32),
            vmem((1, PAIR), F32),
            vmem((8, 8, ROWS), F32),
            vmem((8, ROWS), F32),
            vmem((4, NEGS, DIM), F32),
            vmem((3, NEGS, DIM), BF16),
            vmem((3, NEGS, DIM), BF16),
            vmem((4, ROWS, DIM), F32),
            vmem((3, ROWS, DIM), BF16),
            vmem((2, ROWS // 2, DIM), BF16),
            vmem((2, ROWS, DIM), BF16),
            vmem((4, TALL, PAIR), F32),
            vmem((4, DIM, ROWS), BF16),
            vmem((4, DIM, ROWS), BF16),
            vmem((3, DIM, ROWS), BF16),
            vmem((3, DIM, ROWS), BF16),
            vmem((4, NEGS, DIM), BF16),
            vmem((SLOTS, 4 * NEGS), BF16),
            pltpu.SemaphoreType.DMA((10,)),
            pltpu.SemaphoreType.DMA((80,)),
            pltpu.SemaphoreType.DMA((80,)),
        ],
        compiler_params=pltpu.CompilerParams(
            collective_id=0, has_side_effects=True, vmem_limit_bytes=54 * 2**20
        ),
        cost_estimate=pl.CostEstimate(flops=10 * 2**30, bytes_accessed=4 * 2**20, transcendentals=12 * 2**20),
    )(*args)
    return pl.pallas_call(
        copy_kernel,
        out_shape=out_shape,
        in_specs=[here] * 3,
        out_specs=[far] * 3,
        scratch_shapes=[pltpu.SemaphoreType.DMA((3,))],
        compiler_params=pltpu.CompilerParams(vmem_limit_bytes=2**20),
    )(*results)


def solution(mesh):
    rows = P(("group", "batch"), None)
    flat = P(("group", "batch"))
    in_specs = (rows, rows, flat, flat, flat, rows, flat, flat, flat, flat)
    return jax.shard_map(local, mesh=mesh, in_specs=in_specs, out_specs=(rows, rows, rows), check_vma=False)
```

```python
import math

import jax
import jax.numpy as jnp
from jax import lax
from jax.experimental import pallas as pl
from jax.experimental.pallas import tpu as pltpu
from jax.sharding import PartitionSpec as P

MESH = pl.DeviceIdType.MESH
F32 = jnp.float32
BF16 = jnp.bfloat16
LOG2E = math.log2(math.e)
SCALE = 0.125
FLOOR = -1e30

ROWS = 384
NEGS = 128
CANDS = ROWS + NEGS
PAIR = 2 * ROWS
DIM = 256
SLOTS = 512
CHUNK = 32
TALL = DIM + 16
WIDE = PAIR

DIST = (0, 1, 3, 2)
PLACE = (0, 1, 3, 2)


def tiled(x, count):
    return jnp.concatenate([x] * count, axis=1)


def kernel(
    q_in, pos_in, pos_logq_in, pos_ids_in, weight_in, neg_in, neg_logq_in, neg_ids_in, owner_in, slot_in,
    quer_out, item_out, table_out,
    cands, cands_t, quers, scores, raw_a, raw_b, terms, neg_weights, weights_a, weights_b,
    pos_logq, pos_ids, weight, neg_logq, neg_ids, neg_owner, neg_slot,
    cmeta, qmeta, ymeta, logq_col, id_col, stat, decay, stats, shift,
    neg_part, neg_send, neg_got, item_part, item_send, item_relay, item_got,
    quer_part, sib_send, sib_got, quer_send, quer_got,
    neg_rows, onehot, local_sem, send_sem, recv_sem,
):
    g = lax.axis_index("group")
    b = lax.axis_index("batch")
    z, x, c = b // 8, (b // 2) % 4, b % 2
    my_abs = x * 2 + c

    def along_z(step):
        return {"batch": ((z + step) % 4) * 8 + x * 2 + c}

    def along_x(step, flip=0):
        core = (1 - c) if flip else c
        return {"batch": z * 8 + ((x + step) % 4) * 2 + core}

    def along_y(step):
        return {"group": (g + step) % 4}

    sems = iter(range(80))
    sent = []

    def remote(src, dst, target, k=None):
        k = next(sems) if k is None else k
        return pltpu.make_async_remote_copy(
            src_ref=src, dst_ref=dst, send_sem=send_sem.at[k], recv_sem=recv_sem.at[k],
            device_id=target, device_id_type=MESH,
        )

    def go(copy):
        copy.start()
        sent.append(copy)

    peers = [along_z(s) for s in (1, 2, 3)]
    peers += [along_x(s, f) for s in range(4) for f in range(2) if (s, f) != (0, 0)]
    peers += [along_y(s) for s in (1, 2, 3)]
    barrier = pltpu.get_barrier_semaphore()
    for peer in peers:
        pl.semaphore_signal(barrier, inc=1, device_id=peer, device_id_type=MESH)

    pairs = [
        (q_in, quers.at[0, pl.ds(0, ROWS)]),
        (pos_in, cands.at[0, pl.ds(0, ROWS)]),
        (neg_in, cands.at[0, pl.ds(ROWS, NEGS)]),
        (pos_logq_in, pos_logq), (pos_ids_in, pos_ids), (weight_in, weight),
        (neg_logq_in, neg_logq), (neg_ids_in, neg_ids), (owner_in, neg_owner), (slot_in, neg_slot),
    ]
    locals_ = [pltpu.make_async_copy(src, dst, local_sem.at[k]) for k, (src, dst) in enumerate(pairs)]
    for copy in locals_:
        copy.start()
    for copy in locals_[:3]:
        copy.wait()
    pl.semaphore_wait(barrier, len(peers))
    qh, ch = ROWS // 2, CANDS // 2

    def quer_at(p, half):
        return quers.at[p, pl.ds(half * qh, qh)]

    def cand_at(p, half):
        return cands.at[p, pl.ds(half * ch, ch)]

    sib = [
        remote(quers.at[p, pl.ds(0, ROWS)], quers.at[p, pl.ds(ROWS, ROWS)], along_x(0, 1)) for p in range(4)
    ]
    own_quers = quers.at[0, pl.ds(0, ROWS)]
    quer_up = remote(own_quers, quers.at[1, pl.ds(0, ROWS)], along_x(1))
    quer_down = remote(own_quers, quers.at[2, pl.ds(0, ROWS)], along_x(-1))
    quer_far = [
        remote(quer_at(1, 0), quer_at(3, 0), along_x(1)),
        remote(quer_at(2, 1), quer_at(3, 1), along_x(-1)),
    ]
    cand_up = remote(cands.at[0], cands.at[1], along_z(1))
    cand_down = remote(cands.at[0], cands.at[2], along_z(-1))
    cand_far = [
        remote(cand_at(1, 0), cand_at(3, 0), along_z(1)),
        remote(cand_at(2, 1), cand_at(3, 1), along_z(-1)),
    ]
    go(cand_up)
    go(cand_down)
    go(quer_up)
    go(quer_down)
    go(sib[0])
    for copy in locals_[3:]:
        copy.wait()
    cmeta[0, 0:1, 0:ROWS] = pos_logq[...].astype(F32).reshape(1, ROWS) * LOG2E
    cmeta[0, 0:1, ROWS:CANDS] = neg_logq[...].astype(F32).reshape(1, NEGS) * LOG2E
    cmeta[0, 1:2, 0:ROWS] = pos_ids[...].reshape(1, ROWS).astype(F32)
    cmeta[0, 1:2, ROWS:CANDS] = neg_ids[...].reshape(1, NEGS).astype(F32)
    qmeta[0, 0:1, 0:ROWS] = pos_ids[...].reshape(1, ROWS).astype(F32)
    qmeta[0, 1:2, 0:ROWS] = weight[...].reshape(1, ROWS)
    ymeta[0] = neg_owner[...].reshape(1, NEGS) * SLOTS + neg_slot[...].reshape(1, NEGS)

    def columns(p):
        cands_t[p, 0:DIM, :] = cands[p].T
        for k in range(CANDS // 128):
            lanes = pl.ds(k * 128, 128)
            for row, ref in ((0, logq_col), (1, id_col)):
                ref[p, lanes, :] = jnp.broadcast_to(cmeta[p, row : row + 1, lanes], (128, 128)).T


    qmeta_copies = {}
    for s in range(4):
        for f in range(2):
            if (s, f) != (0, 0):
                place = qmeta.at[PLACE[s], :, pl.ds(f * ROWS, ROWS)]
                qmeta_copies[(PLACE[s], f)] = remote(qmeta.at[0, :, pl.ds(0, ROWS)], place, along_x(s, f))
    cmeta_copies = {PLACE[s]: remote(cmeta.at[0], cmeta.at[PLACE[s]], along_z(s)) for s in (1, 2, 3)}
    ymeta_copies = [remote(ymeta.at[0], ymeta.at[s], along_y(s)) for s in (1, 2, 3)]
    go(qmeta_copies[(0, 1)])
    for key, copy in qmeta_copies.items():
        if key != (0, 1):
            go(copy)
    for copy in (*cmeta_copies.values(), *ymeta_copies):
        go(copy)

    columns(0)
    stat[...] = jnp.full((4, 1, PAIR), FLOOR, F32)
    cands_t[:, DIM:TALL, :] = jnp.ones((4, TALL - DIM, CANDS), BF16)
    quer_part[...] = jnp.zeros_like(quer_part)

    def on_target(r, first=0, width=PAIR):
        r_index = lax.broadcasted_iota(jnp.int32, (CHUNK, width), 0) + r * CHUNK
        q_index = lax.broadcasted_iota(jnp.int32, (CHUNK, width), 1) + first
        return jnp.logical_and(r_index == q_index, q_index < ROWS)

    def score(raw, p, cs, n):
        raw[:, n : n + WIDE] = lax.dot_general(
            cands[cs], quers[p, n : n + WIDE, :], (((1,), (1,)), ((), ())), preferred_element_type=F32
        )

    def fold(p, cs, n):
        quer_part[p, :, n : n + WIDE] = quer_part[p, :, n : n + WIDE] * decay[:, n : n + WIDE] + jnp.dot(
            cands_t[cs], terms[:, n : n + WIDE], preferred_element_type=F32
        )

    def expand(raw, p, cs, n, diagonal=False):
        lanes = slice(n, n + WIDE)
        row_ids = qmeta[p, 0:1, lanes]

        def mask(r, peak):
            rows = pl.ds(pl.multiple_of(r * CHUNK, CHUNK), CHUNK)
            s = raw[rows, lanes] * (SCALE * LOG2E) - tiled(logq_col[cs, rows, :], WIDE // 128)
            drop = tiled(id_col[cs, rows, :], WIDE // 128) == row_ids
            if diagonal:
                drop = jnp.logical_and(drop, jnp.logical_not(on_target(r, n, WIDE)))
            s = jnp.where(drop, FLOOR, s)
            scores[p, cs, rows, lanes] = s
            return jnp.maximum(peak, jnp.max(s.reshape(CHUNK // 8, 8, WIDE), axis=0))

        peak = lax.fori_loop(0, CANDS // CHUNK, mask, jnp.full((8, WIDE), FLOOR, F32), unroll=True)
        old = stat[p, :, lanes]
        new = jnp.maximum(old, jnp.max(peak, axis=0, keepdims=True))

        def add(r, carry):
            rows = pl.ds(pl.multiple_of(r * CHUNK, CHUNK), CHUNK)
            terms[rows, lanes] = jnp.exp2(scores[p, cs, rows, lanes] - new).astype(BF16)
            return carry

        lax.fori_loop(0, CANDS // CHUNK, add, 0, unroll=True)
        decay[:, lanes] = jnp.exp2(old - new)
        stat[p, :, lanes] = new

    def step(now, raw, ahead=None, raw_ahead=None, before=None, diagonal=False):
        for n in range(0, PAIR, WIDE):
            if ahead is not None:
                score(raw_ahead, *ahead, n)
            if before is not None:
                fold(*before, n)
            expand(raw, *now, n, diagonal)

    order = [(p, 0) for p in range(3)] + [(p, cs) for cs in (1, 2) for p in range(3)]
    order += [(3, cs) for cs in range(3)] + [(p, 3) for p in range(4)]

    def candidates_from(p, copies):
        for copy in (*copies, cmeta_copies[p]):
            copy.wait_recv()
        columns(p)

    def queries_from(p):
        sib[p].wait_recv()
        for f in (0, 1):
            qmeta_copies[(p, f)].wait_recv()

    sib[0].wait_recv()
    qmeta_copies[(0, 1)].wait_recv()
    for n in range(0, PAIR, WIDE):
        score(raw_a, 0, 0, n)
    step((0, 0), raw_a, diagonal=True)
    quer_up.wait_recv()
    go(sib[1])
    quer_down.wait_recv()
    go(sib[2])
    go(quer_far[0])
    go(quer_far[1])
    cand_up.wait_recv()
    go(cand_far[0])
    cand_down.wait_recv()
    go(cand_far[1])
    queries_from(1)
    score(raw_b, 1, 0, 0)
    raws = (raw_a, raw_b)
    for t in range(1, 16):
        ahead = order[t + 1] if t < 15 else None
        if ahead == (2, 0):
            queries_from(2)
        elif ahead == (0, 1):
            candidates_from(1, ())
        elif ahead == (0, 2):
            candidates_from(2, ())
            quer_far[0].wait_recv()
            quer_far[1].wait_recv()
            go(sib[3])
        elif ahead == (3, 0):
            queries_from(3)
        elif ahead == (0, 3):
            candidates_from(3, cand_far)
        step(order[t], raws[t % 2], ahead, raws[(t + 1) % 2], order[t - 1])
    fold(*order[15], 0)

    def owner(p, f):
        core = (1 - c) if f else c
        return ((x + 4 - DIST[p]) % 4) * 2 + core

    def count(p):
        return quer_part[p, DIM : DIM + 1, :]

    for p in range(4):
        part = stat[p] + jnp.log(count(p)) * LOG2E
        for f in range(2):
            stats[my_abs, pl.ds(owner(p, f), 1), :] = part[:, f * ROWS : (f + 1) * ROWS]
    stat_copies = {}
    for s in (2, 1, 3, 0):
        for f in range(2):
            if (s, f) != (0, 0):
                j = next(sems)
                go(remote(stats.at[my_abs], stats.at[my_abs], along_x(s, f), j))
                k = owner(PLACE[s], f)
                stat_copies[(s, f)] = remote(stats.at[k], stats.at[k], along_x(s, f), j)

    sib_parts = [remote(sib_send.at[p], sib_got.at[p], along_x(0, 1)) for p in range(4)]
    for p in (3, 1, 2, 0):
        share = 1.0 / count(p)[:, ROWS:PAIR]
        sib_send[p] = (quer_part[p, 0:DIM, ROWS:PAIR] * share).astype(BF16)
        go(sib_parts[p])
    stat_copies[(0, 1)].wait_recv()

    def chip_average(p):
        row = pl.ds(owner(p, 0), 1)
        mine, other = stats[my_abs, row, :], stats[owner(0, 1), row, :]
        top = jnp.maximum(mine, other)
        mine, other = jnp.exp2(mine - top), jnp.exp2(other - top)
        both = 1.0 / (mine + other)
        mine, other = mine * both / count(p)[:, 0:ROWS], other * both
        return quer_part[p, 0:DIM, 0:ROWS] * mine + sib_got[p].astype(F32) * other

    quer_copies = []
    for p, step_x in ((3, 2), (1, -1), (2, 1)):
        sib_parts[p].wait_recv()
        quer_send[p - 1] = chip_average(p).astype(BF16)
        copy = remote(quer_send.at[p - 1], quer_got.at[p - 1], along_x(step_x))
        go(copy)
        quer_copies.append(copy)
    for copy in ymeta_copies:
        copy.wait_recv()
    for k in range(4):
        want = lax.broadcasted_iota(jnp.int32, (SLOTS, NEGS), 0) + g * SLOTS
        onehot[:, k * NEGS : (k + 1) * NEGS] = jnp.where(ymeta[k] == want, 1.0, 0.0).astype(BF16)
    for key, copy in stat_copies.items():
        if key != (0, 1):
            copy.wait_recv()
    peak = stats[0]
    for k in range(1, 8):
        peak = jnp.maximum(peak, stats[k])
    total = jnp.zeros_like(peak)
    for k in range(8):
        total = total + jnp.exp2(stats[k] - peak)
    shift[...] = peak + jnp.log(total) * LOG2E
    lifts = []
    for p in range(4):
        lse = jnp.concatenate([shift[pl.ds(owner(p, f), 1), :] for f in range(2)], axis=1)
        lifts.append(jnp.log(qmeta[p, 1:2, :]) * LOG2E - lse)

    def weigh(cs, r, out, place):
        rows = pl.ds(pl.multiple_of(r * CHUNK, CHUNK), CHUNK)
        for p in range(4):
            gw = jnp.exp2(scores[p, cs, rows, :] + lifts[p])
            if p == 0 and cs == 0:
                gw = jnp.where(on_target(r), gw - qmeta[0, 1:2, :], gw)
            out[place, p * PAIR : (p + 1) * PAIR] = gw.astype(BF16)

    all_quers = quers[...].reshape(4 * PAIR, DIM)

    def weigh_items(cs, out):
        def do(r, carry):
            weigh(cs, r, out, pl.ds(pl.multiple_of(r * CHUNK, CHUNK), CHUNK))
            return carry

        lax.fori_loop(0, ROWS // CHUNK, do, 0, unroll=True)

    neg_copies = []
    steps_z = {3: 2, 1: -1, 2: 1}
    for group in ((2, 3), (0, 1)):
        for cs in group:
            for r in range(NEGS // CHUNK):
                weigh(cs, ROWS // CHUNK + r, neg_weights, pl.ds(cs * NEGS + r * CHUNK, CHUNK))
        first, count_rows = min(group), len(group) * NEGS
        neg_part[first : first + len(group)] = jnp.dot(
            neg_weights[first * NEGS : first * NEGS + count_rows, :], all_quers, preferred_element_type=F32
        ).reshape(len(group), NEGS, DIM)
        if 0 in group:
            weigh_items(3, weights_a)
        for cs in group:
            if cs:
                neg_send[cs - 1] = neg_part[cs].astype(BF16)
                copy = remote(neg_send.at[cs - 1], neg_got.at[cs - 1], along_z(steps_z[cs]))
                go(copy)
                neg_copies.append(copy)

    def item_block(cs, held, after=None, out=None):
        item_part[cs] = jnp.dot(held[...], all_quers, preferred_element_type=F32)
        if out is not None:
            weigh_items(after, out)

    ih = ROWS // 2
    up, low = pl.ds(0, ih), pl.ds(ih, ih)
    relay_copies = [
        remote(item_send.at[2, up], item_relay.at[0], along_z(-1)),
        remote(item_send.at[2, low], item_relay.at[1], along_z(1)),
    ]
    to_down = [remote(item_send.at[0, h], item_got.at[0, h], along_z(-1)) for h in (up, low)]
    to_up = [remote(item_send.at[1, h], item_got.at[1, h], along_z(1)) for h in (up, low)]
    item_block(3, weights_a, 1, weights_b)
    item_send[2] = item_part[3].astype(BF16)
    go(relay_copies[1])
    go(relay_copies[0])
    item_block(1, weights_b, 2, weights_a)
    item_send[0, low, :] = item_part[1, low, :].astype(BF16)
    go(to_down[1])
    item_block(2, weights_a, 0, weights_b)
    item_send[1, up, :] = item_part[2, up, :].astype(BF16)
    go(to_up[0])
    item_block(0, weights_b)
    for copy in neg_copies:
        copy.wait_recv()
    neg_rows[0] = (
        neg_part[0] + neg_got[0].astype(F32) + neg_got[1].astype(F32) + neg_got[2].astype(F32)
    ).astype(BF16)
    y_copies = [remote(neg_rows.at[0], neg_rows.at[s], along_y(s)) for s in (2, 1, 3)]
    for copy in y_copies:
        go(copy)
    relay_copies[1].wait_recv()
    item_send[1, low, :] = (item_part[2, low, :] + item_relay[1].astype(F32)).astype(BF16)
    go(to_up[1])
    relay_copies[0].wait_recv()
    item_send[0, up, :] = (item_part[1, up, :] + item_relay[0].astype(F32)).astype(BF16)
    go(to_down[0])

    my_row = pl.ds(my_abs, 1)

    def chip_weight(step):
        k = ((x + step) % 4) * 2
        return sum(jnp.exp2(stats[k + f, my_row, :] - shift[my_row, :]) for f in range(2))

    sib_parts[0].wait_recv()
    own = chip_average(0) * chip_weight(0)
    for k, step_x in ((2, 2), (0, 1), (1, 3)):
        quer_copies[(1, 2, 0)[k]].wait_recv()
        own = own + quer_got[k].astype(F32) * chip_weight(step_x)
    own = (own - cands_t[0, 0:DIM, 0:ROWS].astype(F32)) * qmeta[0, 1:2, 0:ROWS]
    quer_out[...] = (own * SCALE).T
    for copy in y_copies:
        copy.wait_recv()
    table_out[...] = SCALE * jnp.dot(
        onehot[...], neg_rows[...].reshape(4 * NEGS, DIM), preferred_element_type=F32
    )
    for copy in (*to_down, *to_up):
        copy.wait_recv()
    item_out[...] = SCALE * (item_part[0] + item_got[0].astype(F32) + item_got[1].astype(F32))
    for copy in sent:
        copy.wait_send()


def copy_kernel(*refs):
    sems = refs[-1]
    copies = [pltpu.make_async_copy(refs[k], refs[3 + k], sems.at[k]) for k in range(3)]
    for copy in copies:
        copy.start()
    for copy in copies:
        copy.wait()


def local(*args):
    far = pl.BlockSpec(memory_space=pl.ANY)
    here = pl.BlockSpec(memory_space=pltpu.VMEM)
    vmem = pltpu.VMEM
    out_shape = [
        jax.ShapeDtypeStruct((ROWS, DIM), F32),
        jax.ShapeDtypeStruct((ROWS, DIM), F32),
        jax.ShapeDtypeStruct((SLOTS, DIM), F32),
    ]
    results = pl.pallas_call(
        kernel,
        out_shape=[pltpu.VMEM(o.shape, o.dtype) for o in out_shape],
        in_specs=[far] * 10,
        out_specs=[here] * 3,
        scratch_shapes=[
            vmem((4, CANDS, DIM), BF16),
            vmem((4, TALL, CANDS), BF16),
            vmem((4, PAIR, DIM), BF16),
            vmem((4, 4, CANDS, PAIR), F32),
            vmem((CANDS, PAIR), F32),
            vmem((CANDS, PAIR), F32),
            vmem((CANDS, PAIR), BF16),
            vmem((4 * NEGS, 4 * PAIR), BF16),
            vmem((ROWS, 4 * PAIR), BF16),
            vmem((ROWS, 4 * PAIR), BF16),
            vmem((ROWS,), BF16), vmem((ROWS,), jnp.int32), vmem((ROWS,), F32),
            vmem((NEGS,), BF16), vmem((NEGS,), jnp.int32), vmem((NEGS,), jnp.int32), vmem((NEGS,), jnp.int32),
            vmem((4, 2, CANDS), F32),
            vmem((4, 2, PAIR), F32),
            vmem((4, 1, NEGS), jnp.int32),
            vmem((4, CANDS, 128), F32),
            vmem((4, CANDS, 128), F32),
            vmem((4, 1, PAIR), F32),
            vmem((1, PAIR), F32),
            vmem((8, 8, ROWS), F32),
            vmem((8, ROWS), F32),
            vmem((4, NEGS, DIM), F32),
            vmem((3, NEGS, DIM), BF16),
            vmem((3, NEGS, DIM), BF16),
            vmem((4, ROWS, DIM), F32),
            vmem((3, ROWS, DIM), BF16),
            vmem((2, ROWS // 2, DIM), BF16),
            vmem((2, ROWS, DIM), BF16),
            vmem((4, TALL, PAIR), F32),
            vmem((4, DIM, ROWS), BF16),
            vmem((4, DIM, ROWS), BF16),
            vmem((3, DIM, ROWS), BF16),
            vmem((3, DIM, ROWS), BF16),
            vmem((4, NEGS, DIM), BF16),
            vmem((SLOTS, 4 * NEGS), BF16),
            pltpu.SemaphoreType.DMA((10,)),
            pltpu.SemaphoreType.DMA((80,)),
            pltpu.SemaphoreType.DMA((80,)),
        ],
        compiler_params=pltpu.CompilerParams(
            collective_id=0, has_side_effects=True, vmem_limit_bytes=54 * 2**20
        ),
        cost_estimate=pl.CostEstimate(flops=10 * 2**30, bytes_accessed=4 * 2**20, transcendentals=12 * 2**20),
    )(*args)
    return pl.pallas_call(
        copy_kernel,
        out_shape=out_shape,
        in_specs=[here] * 3,
        out_specs=[far] * 3,
        scratch_shapes=[pltpu.SemaphoreType.DMA((3,))],
        compiler_params=pltpu.CompilerParams(vmem_limit_bytes=2**20),
    )(*results)


def solution(mesh):
    rows = P(("group", "batch"), None)
    flat = P(("group", "batch"))
    in_specs = (rows, rows, flat, flat, flat, rows, flat, flat, flat, flat)
    return jax.shard_map(local, mesh=mesh, in_specs=in_specs, out_specs=(rows, rows, rows), check_vma=False)
```
